128 devices in a mesh: sec: 4 (over y), dev: 32 (over z, x, core).
Axes of the slice: x: 4, y: 4, z: 4, core: 2. Of those that a mesh axis runs over, the one named last changes fastest.
Arguments:
- query: bfloat16 [256, 8192], P(('sec', 'dev')), may hold values from -160 to 160
- fresh_key_value: bfloat16 [256, 4, 256], P(('sec', 'dev')), may hold values from -6 to 6
- kv_cache: bfloat16 [256, 1024, 4, 256], P(('sec', 'dev')), may hold values from -6 to 6
- cache_lengths: int32 [256], P(('sec', 'dev')), may hold values from 2 to 1024, as said below
- hidden: bfloat16 [1536, 4096], P(('sec', 'dev')), may hold values from -6 to 6
- routes: int32 [1536, 8], P(('sec', 'dev')), may hold values from 0 to 15, all different within a row; in each aligned block of 12 rows (0 to 11, 12 to 23, ...) at most 9 rows name the same one
- gates: float32 [1536, 8], P(('sec', 'dev')), may hold values from 0.05 to 1
- w_gate_up: bfloat16 [128, 4096, 1536], P(('sec', 'dev')), may hold values from -0.09375 to 0.09375
- w_down: bfloat16 [128, 768, 4096], P(('sec', 'dev')), may hold values from -0.15625 to 0.15625
Outputs:
- attention_out: bfloat16 [256, 8192], P(('sec', 'dev'))
- moe_out: bfloat16 [1536, 4096], P(('sec', 'dev'))
The draws below stay inside these ranges and needn't reach their ends.
Inputs may be any that keep to these rules, and one draw needn't show every extreme that they name: `cache_lengths`: one served request holds all 1024 entries. `routes`: each row names 8 different experts; among the 12 rows of one device no expert is named more than 9 times.
All inputs are finite; a program needn't handle non-finite values.
Results may differ from the reference program's by a relative error of at most 0.005.
Values may be sent and summed in bfloat16 or wider, within the bound.
No kernel may reach another device: no remote copies, remote signals or barrier semaphores. Data moves between devices by JAX's collectives and lax.ppermute only.
A program may use at most 128 MiB of HBM per device.

```python
import math
import jax
import jax.numpy as jnp
import numpy as np
from jax import lax

D = 4096
FI = 1536
QUERY_HEAD_COUNT = 64
KEY_VALUE_HEADS = 4
HEAD_WIDTH = 128
REQ_DEV = 2
CACHE_LENGTH = 1024
TOK_DEV = 12
ATT_DEVICES = 96
GROUP_QUERIES = 16
FIH = 768
EXPERTS = 16
TOPK = 8
CAP = 9
REQUEST_SLOTS = 256
TOKENS = 1536
DEVICES = 128


def leading_keys(key):
    return jnp.clip(jax.random.normal(jax.random.fold_in(key, 101), (REQUEST_SLOTS, 2, KEY_VALUE_HEADS, HEAD_WIDTH), jnp.float32), -6.0, 6.0)


def draw_kv_cache(key, part):
    leading = leading_keys(key)
    key = jax.random.fold_in(key, 3)
    kv_cache_block = jnp.clip(jax.random.normal(key, (REQUEST_SLOTS, CACHE_LENGTH, KEY_VALUE_HEADS, 2 * HEAD_WIDTH), jnp.float32), -6.0, 6.0)
    kv_cache_block = kv_cache_block.at[:, 0:2, :, 0:HEAD_WIDTH].set(leading)
    return kv_cache_block.astype(jnp.bfloat16)


def draw_query(key, part):
    key = jax.random.fold_in(key, 5)
    query_rows = jnp.clip(jax.random.normal(key, (REQUEST_SLOTS, KEY_VALUE_HEADS, GROUP_QUERIES, HEAD_WIDTH), jnp.float32), -6.0, 6.0)
    return query_rows.reshape(REQUEST_SLOTS, QUERY_HEAD_COUNT * HEAD_WIDTH).astype(jnp.bfloat16)


def draw_cache_lengths(key, part):
    key = jax.random.fold_in(key, 13)
    first_draw = jax.random.randint(jax.random.fold_in(key, 1), (REQUEST_SLOTS,), 2, CACHE_LENGTH + 1)
    second_draw = jax.random.randint(jax.random.fold_in(key, 2), (REQUEST_SLOTS,), 2, CACHE_LENGTH + 1)
    third_draw = jax.random.randint(jax.random.fold_in(key, 3), (REQUEST_SLOTS,), 2, CACHE_LENGTH + 1)
    lengths = jnp.minimum(first_draw, jnp.minimum(second_draw, third_draw))
    longest = jax.random.randint(jax.random.fold_in(key, 17), (), 0, ATT_DEVICES * REQ_DEV)
    lengths = jnp.where(jnp.arange(REQUEST_SLOTS) == longest, CACHE_LENGTH, lengths)
    return lengths.astype(jnp.int32)


def block_levels(own_key, extent, cuts, low, largest):
    gain, own = 1.0, jax.random.fold_in(own_key, 6)
    for position, parts in cuts:
        steps = jnp.exp(jax.random.uniform(jax.random.fold_in(own, position), (parts,), jnp.float32, low / len(cuts), largest / len(cuts)))
        gain = gain * jnp.repeat(steps, extent[position] // parts).reshape([-1 if axis == position else 1 for axis in range(len(extent))])
    return gain


def assign_block(rng, own, number, rows, amount, top, limit, slope):
    ranking = jax.random.permutation(rng, amount)
    heavy_load, common = portions_of(amount, rows * top, limit, slope, True), portions_of(amount, rows * top, limit, slope, False)
    places = jnp.arange(amount)

    def named(sizes, offset_by):
        used = int((sizes > 0).sum())
        fixed = max(1, used // 4)
        moved = fixed + (places - fixed + offset_by * (used - fixed)) % max(1, amount - fixed)
        return jnp.zeros((amount,), jnp.int32).at[ranking[jnp.where(places < fixed, places, moved)]].set(jnp.asarray(sizes, jnp.int32))

    sizes = jnp.where(number % 4 == 0, named(heavy_load, number // 4), named(common, number - number // 4 - 1))
    mixed = jax.random.permutation(jax.random.fold_in(own, 3), amount)
    giver, taker = mixed[0:amount // 2 * 2:2], mixed[1:amount // 2 * 2:2]
    margin = jnp.minimum(sizes[giver] - 1, limit - sizes[taker]) // 2
    margin = jnp.where((giver == ranking[0]) | (taker == ranking[0]) | (sizes[taker] == 0), 0, jnp.maximum(margin, 0))
    moved = jax.random.randint(jax.random.fold_in(own, 4), (amount // 2,), 0, 1 << 20) % (margin + 1)
    sizes = sizes.at[giver].add(-moved).at[taker].add(moved)
    members = jnp.searchsorted(jnp.cumsum(sizes), jnp.arange(rows * top), side="right").astype(jnp.int32)
    table = members.reshape(top, rows).T
    table = table[jax.random.permutation(jax.random.fold_in(own, 1), rows)]
    offset_by = jax.random.randint(jax.random.fold_in(own, 2), (rows, 1), 0, top)
    return jnp.take_along_axis(table, (jnp.arange(top)[None, :] + offset_by) % top, axis=1)


def portions_of(count, total, limit, skew, full):
    weights = [(1 << 20) // math.isqrt(grade ** skew) + 1 for grade in range(1, count + 1)]
    largest = limit if full else min(limit, max(-(-total // count), total * weights[0] // sum(weights)))
    least = 1 if total - largest >= count - 1 else 0
    given, rest = [largest] + [least] * (count - 1), total - largest - least * (count - 1)
    while rest > 0:
        free = [i for i in range(1, count) if given[i] < largest] or [i for i in range(1, count) if given[i] < limit]
        pool, remaining = sum([weights[i] for i in free]), rest
        for i in free:
            addition = min(limit - given[i], max(1, remaining * weights[i] // pool), rest)
            given[i] = given[i] + addition
            rest = rest - addition
    return np.array(given)


def noise(own_key, extent, scale, bound, shards=(), kind=jnp.bfloat16):
    array = jax.random.normal(own_key, extent, jnp.float32) * scale
    if len(shards) > 0:
        array = block_levels(own_key, extent, shards, -0.22, 0.18) * array
    return jnp.clip(array, min=-bound, max=bound).astype(kind)


def setup_inputs(seed: int = 0) -> dict:
    keys = jax.random.split(jax.random.key(seed), 10)
    query = draw_query(jax.random.fold_in(keys[9], 71), 0)
    fresh_key_value = noise(keys[1], (REQUEST_SLOTS, KEY_VALUE_HEADS, 2 * HEAD_WIDTH), 1.0, 6.0, ((0, 128),))
    kv_cache = draw_kv_cache(jax.random.fold_in(keys[9], 71), 0)
    cache_lengths = draw_cache_lengths(jax.random.fold_in(keys[9], 71), 0)
    hidden = noise(keys[4], (TOKENS, D), 1.0, 6.0, ((0, 128),))
    routes_keys = jax.random.split(jax.random.fold_in(keys[5], 1), TOKENS // TOK_DEV)
    routes_turns = jax.random.permutation(jax.random.fold_in(keys[5], 3), TOKENS // TOK_DEV)
    routes = jax.vmap(lambda own, number: assign_block(jax.random.fold_in(keys[5], 2), own, number, TOK_DEV, EXPERTS, TOPK, CAP, 2))(routes_keys, routes_turns).reshape((TOKENS, TOPK))
    gates = jnp.clip(jnp.exp(math.log(1.0) - 2.9957323 * jax.random.uniform(keys[6], (TOKENS, TOPK), jnp.float32) ** block_levels(keys[6], (TOKENS, TOPK), ((0, 128),), -0.2, 0.2)), 0.05, 1.0)
    w_gate_up = noise(keys[7], (DEVICES, D, FI), D ** -0.5, 0.09375, ((0, 128),))
    w_down = noise(keys[8], (DEVICES, FIH, D), FI ** -0.5, 0.15625, ((0, 128),))
    return dict(query=query, fresh_key_value=fresh_key_value, kv_cache=kv_cache, cache_lengths=cache_lengths, hidden=hidden, routes=routes, gates=gates, w_gate_up=w_gate_up, w_down=w_down)


def attend(item):
    single_query, new_row, cache_row, length = item
    query_float = single_query.astype(jnp.float32).reshape(KEY_VALUE_HEADS, QUERY_HEAD_COUNT // KEY_VALUE_HEADS, HEAD_WIDTH)
    key_part = cache_row[:, :, :HEAD_WIDTH].astype(jnp.float32)
    value_part = cache_row[:, :, HEAD_WIDTH:].astype(jnp.float32)
    new_key = new_row[:, :HEAD_WIDTH].astype(jnp.float32)
    new_value = new_row[:, HEAD_WIDTH:].astype(jnp.float32)
    score_scale = HEAD_WIDTH ** -0.5
    scores = jnp.einsum("ghd,tgd->ght", query_float, key_part) * score_scale
    valid = jnp.arange(CACHE_LENGTH, dtype=jnp.int32) < length
    scores = jnp.where(valid[None, None, :], scores, -jnp.inf)
    own_score = jnp.einsum("ghd,gd->gh", query_float, new_key) * score_scale
    peak = jnp.maximum(jnp.max(scores, axis=-1), own_score)
    weights = jnp.exp(scores - peak[..., None])
    own_weight = jnp.exp(own_score - peak)
    denominator = jnp.sum(weights, axis=-1) + own_weight
    weights_low = lax.optimization_barrier(weights.astype(jnp.bfloat16)).astype(jnp.float32)
    own_low = lax.optimization_barrier(own_weight.astype(jnp.bfloat16)).astype(jnp.float32)
    mixture = jnp.einsum("ght,tgd->ghd", weights_low, value_part) + own_low[..., None] * new_value[:, None, :]
    return (mixture / denominator[..., None]).astype(jnp.bfloat16).reshape(QUERY_HEAD_COUNT * HEAD_WIDTH)


def reference(query, fresh_key_value, kv_cache, cache_lengths, hidden, routes, gates, w_gate_up, w_down):
    served_req = ATT_DEVICES * REQ_DEV
    served = lax.map(attend, (query[:served_req], fresh_key_value[:served_req], kv_cache[:served_req], cache_lengths[:served_req]))
    attention_out = jnp.concatenate((served, jnp.zeros((REQUEST_SLOTS - served_req, QUERY_HEAD_COUNT * HEAD_WIDTH), jnp.bfloat16)), axis=0)
    served_tok = ATT_DEVICES * TOK_DEV
    tok_hidden = hidden[:served_tok]
    tok_routes = routes[:served_tok]
    tok_gates = gates[:served_tok]
    combine = tok_gates / jnp.sum(tok_gates, axis=1, keepdims=True)
    slots_max = ATT_DEVICES * CAP

    def expert_pass(running, expert):
        matches = tok_routes == expert
        weight_sum = jnp.sum(jnp.where(matches, combine, 0.0), axis=1)
        chosen = jnp.any(matches, axis=1)
        picked = jnp.nonzero(chosen, size=slots_max, fill_value=0)[0].astype(jnp.int32)
        occupied = jnp.arange(slots_max, dtype=jnp.int32) < jnp.sum(chosen.astype(jnp.int32))
        gathered = tok_hidden[picked]
        expert_y = jnp.zeros((slots_max, D), jnp.float32)
        for which in range(2):
            row_index = ATT_DEVICES + 2 * expert + which
            gate_up = lax.dynamic_index_in_dim(w_gate_up, row_index, 0, keepdims=False)
            down_weight = lax.dynamic_index_in_dim(w_down, row_index, 0, keepdims=False)
            projected = jnp.dot(gathered, gate_up, preferred_element_type=jnp.float32)
            activated = (jax.nn.silu(projected[:, :FIH]) * projected[:, FIH:]).astype(jnp.bfloat16)
            expert_y = expert_y + jnp.dot(activated, down_weight, preferred_element_type=jnp.float32)
        scaling = jnp.where(occupied, weight_sum[picked], 0.0)
        contribution = expert_y * scaling[:, None]
        return running.at[picked].add(contribution), None

    summed, _ = lax.scan(expert_pass, jnp.zeros((served_tok, D), jnp.float32), jnp.arange(EXPERTS, dtype=jnp.int32))
    moe_out = jnp.concatenate((summed.astype(jnp.bfloat16), jnp.zeros((TOKENS - served_tok, D), jnp.bfloat16)), axis=0)
    return attention_out, moe_out
```

```python
import jax
import jax.numpy as jnp
from jax import lax
from jax.sharding import PartitionSpec as P

SIDE = 4
EXTRA = 128


def along(first, distance):
    pairs = []
    for i in range(2 * SIDE * SIDE):
        z, x, core = i // (2 * SIDE), i // 2 % SIDE, i % 2
        if first == (core == 0):
            x = (x + distance) % SIDE
        else:
            z = (z + distance) % SIDE
        pairs.append((i, (z * SIDE + x) * 2 + core))
    return pairs


def step_u(block, distance):
    return lax.ppermute(block, "dev", along(True, distance))


def step_v(block, distance):
    return lax.ppermute(block, "dev", along(False, distance))


def step_sec(block, distance):
    return lax.ppermute(block, "sec", [(i, (i + distance) % SIDE) for i in range(SIDE)])


def other_core(block):
    return lax.ppermute(block, "dev", [(i, i ^ 1) for i in range(2 * SIDE * SIDE)])


def attention_block(query, fresh_key_value, kv_cache, cache_lengths):
    count_req = query.shape[0]
    heads_kv = fresh_key_value.shape[1]
    head_size = fresh_key_value.shape[2] // 2
    group_size = query.shape[1] // (heads_kv * head_size)
    query_heads = query.reshape(count_req, heads_kv, group_size, head_size)
    score_scale = head_size ** (-0.5)
    scores = (
        jnp.einsum(
            "rghd,rtgd->rght",
            query_heads,
            kv_cache[..., :head_size],
            preferred_element_type=jnp.float32,
        )
        * score_scale
    )
    valid = jnp.arange(kv_cache.shape[1], dtype=jnp.int32)[None, :] < cache_lengths[:, None]
    scores = jnp.where(valid[:, None, None, :], scores, -jnp.inf)
    own_score = (
        jnp.einsum(
            "rghd,rgd->rgh",
            query_heads,
            fresh_key_value[..., :head_size],
            preferred_element_type=jnp.float32,
        )
        * score_scale
    )
    peak = jnp.maximum(jnp.max(scores, axis=-1), own_score)
    weights = jnp.exp(scores - peak[..., None])
    own_weight = jnp.exp(own_score - peak)
    denominator = jnp.sum(weights, axis=-1) + own_weight
    own_low = lax.optimization_barrier(own_weight.astype(jnp.bfloat16)).astype(jnp.float32)
    mixture = jnp.einsum(
        "rght,rtgd->rghd",
        weights.astype(jnp.bfloat16),
        kv_cache[..., head_size:],
        preferred_element_type=jnp.float32,
    )
    mixture = (
        mixture
        + own_low[..., None] * fresh_key_value[..., head_size:].astype(jnp.float32)[:, :, None, :]
    )
    return (mixture / denominator[..., None]).astype(jnp.bfloat16).reshape(count_req, -1)


def token_rows(hidden, routes, gates, experts):
    combine = gates / jnp.sum(gates, axis=1, keepdims=True)
    named = routes[:, :, None] == jnp.arange(experts, dtype=jnp.int32)[None, None, :]
    share = jnp.sum(jnp.where(named, combine[:, :, None], 0.0), axis=1)
    terms = []
    for _ in range(3):
        term = lax.reduce_precision(share, 8, 7)
        terms.append(term.astype(jnp.bfloat16))
        share = share - term
    fill = jnp.zeros((hidden.shape[0], EXTRA - 3 * experts), jnp.bfloat16)
    return jnp.concatenate([hidden, *terms, fill], axis=1)


def experts_on(rows, picks, weights):
    width = rows.shape[1] - EXTRA
    share = jnp.sum(
        jnp.where(picks, rows[:, width:].astype(jnp.float32), 0.0), axis=1, keepdims=True
    )
    total = None
    for gate_up, down in weights:
        inner = down.shape[0]
        projected = jnp.dot(rows[:, :width], gate_up, preferred_element_type=jnp.float32)
        act = (jax.nn.silu(projected[:, :inner]) * projected[:, inner:]).astype(jnp.bfloat16)
        part = jnp.dot(act, down, preferred_element_type=jnp.float32)
        total = part if total is None else total + part
    return (total * share).astype(jnp.bfloat16)


def per_device(
    query, fresh_key_value, kv_cache, cache_lengths, hidden, routes, gates, w_gate_up, w_down
):
    sections = lax.axis_size("sec")
    section = lax.axis_index("sec")
    experts = lax.axis_size("dev") // 2
    expert = lax.axis_index("dev") // 2
    expert_side = section == sections - 1
    count = hidden.shape[0]
    f32 = jnp.float32

    gate_up, down = w_gate_up[0], w_down[0]
    weights = ((gate_up, down), (other_core(gate_up), other_core(down)))

    packed = token_rows(hidden, routes, gates, experts)
    block = jnp.concatenate([step_sec(packed, sections - 1 - s) for s in range(sections - 1)], axis=0)

    group = jnp.concatenate([block, step_u(block, 1), step_u(block, -1), step_u(block, 2)], axis=0)
    before, after = step_v(group, 1), step_v(group, -1)
    half = group.shape[0] // 2
    across = jnp.concatenate([step_v(before[:half], 1), step_v(after[half:], -1)], axis=0)

    attention_out = attention_block(query, fresh_key_value, kv_cache, cache_lengths)
    attention_out = jnp.where(expert_side, jnp.zeros_like(attention_out), attention_out)

    column = lax.broadcasted_iota(jnp.int32, (1, EXTRA), 1)
    picks = (column % experts == expert) & (column < 3 * experts)
    size = group.shape[0]
    y_one = experts_on(jnp.concatenate([group, before], axis=0), picks, weights)
    y_two = experts_on(jnp.concatenate([after, across], axis=0), picks, weights)
    y_own, y_before, y_after, y_across = y_one[:size], y_one[size:], y_two[:size], y_two[size:]

    to_after, to_before = step_v(y_across[:half], 1), step_v(y_across[half:], -1)
    y_after = jnp.concatenate(
        [(y_after[:half].astype(f32) + to_after.astype(f32)).astype(jnp.bfloat16), y_after[half:]], axis=0
    )
    y_before = jnp.concatenate(
        [y_before[:half], (y_before[half:].astype(f32) + to_before.astype(f32)).astype(jnp.bfloat16)], axis=0
    )
    summed = y_own.astype(f32) + step_v(y_after, 1).astype(f32) + step_v(y_before, -1).astype(f32)
    held = sections * count - count
    low = summed.astype(jnp.bfloat16)
    total = (
        summed[:held]
        + step_u(low[held : 2 * held], -1).astype(f32)
        + step_u(low[2 * held : 3 * held], 1).astype(f32)
        + step_u(low[3 * held :], 2).astype(f32)
    ).astype(jnp.bfloat16)

    result = jnp.zeros((count, total.shape[1]), jnp.bfloat16)
    for s in range(sections - 1):
        back = step_sec(total[s * count : (s + 1) * count], s + 1)
        result = jnp.where(section == s, back, result)
    return attention_out, result


def solution(mesh):
    return jax.shard_map(
        per_device,
        mesh=mesh,
        in_specs=(
            P(("sec", "dev"), None),
            P(("sec", "dev"), None, None),
            P(("sec", "dev"), None, None, None),
            P(("sec", "dev")),
            P(("sec", "dev"), None),
            P(("sec", "dev"), None),
            P(("sec", "dev"), None),
            P(("sec", "dev"), None, None),
            P(("sec", "dev"), None, None),
        ),
        out_specs=(P(("sec", "dev"), None), P(("sec", "dev"), None)),
        check_vma=False,
    )
```

```python
import functools

import jax
import jax.numpy as jnp
from jax import lax
from jax.experimental import pallas as pl
from jax.experimental.pallas import tpu as pltpu
from jax.sharding import PartitionSpec as P

SIDE = 4
EXTRA = 128


def along(first, distance):
    pairs = []
    for i in range(2 * SIDE * SIDE):
        z, x, core = i // (2 * SIDE), i // 2 % SIDE, i % 2
        if first == (core == 0):
            x = (x + distance) % SIDE
        else:
            z = (z + distance) % SIDE
        pairs.append((i, (z * SIDE + x) * 2 + core))
    return pairs


def step_u(block, distance):
    return lax.ppermute(block, "dev", along(True, distance))


def step_v(block, distance):
    return lax.ppermute(block, "dev", along(False, distance))


def to_section(block, source, target):
    return lax.ppermute(block, "sec", [(source, target)])


def stacked(blocks):
    rows = sum(block.shape[0] for block in blocks)
    start, total = 0, None
    for block in blocks:
        size = block.shape[0]
        padded = jnp.pad(block, ((start, rows - start - size), (0, 0)))
        total = padded if total is None else total + padded
        start += size
    return total


def other_core(block):
    return lax.ppermute(block, "dev", [(i, i ^ 1) for i in range(2 * SIDE * SIDE)])


def attention_block(query, fresh_key_value, kv_cache, cache_lengths):
    count_req = query.shape[0]
    heads_kv = fresh_key_value.shape[1]
    head_size = fresh_key_value.shape[2] // 2
    group_size = query.shape[1] // (heads_kv * head_size)
    query_heads = query.reshape(count_req, heads_kv, group_size, head_size)
    score_scale = head_size ** (-0.5)
    scores = (
        jnp.einsum(
            "rghd,rtgd->rght",
            query_heads,
            kv_cache[..., :head_size],
            preferred_element_type=jnp.float32,
        )
        * score_scale
    )
    valid = jnp.arange(kv_cache.shape[1], dtype=jnp.int32)[None, :] < cache_lengths[:, None]
    scores = jnp.where(valid[:, None, None, :], scores, -jnp.inf)
    own_score = (
        jnp.einsum(
            "rghd,rgd->rgh",
            query_heads,
            fresh_key_value[..., :head_size],
            preferred_element_type=jnp.float32,
        )
        * score_scale
    )
    peak = jnp.maximum(jnp.max(scores, axis=-1), own_score)
    weights = jnp.exp(scores - peak[..., None])
    own_weight = jnp.exp(own_score - peak)
    denominator = jnp.sum(weights, axis=-1) + own_weight
    own_low = lax.optimization_barrier(own_weight.astype(jnp.bfloat16)).astype(jnp.float32)
    mixture = jnp.einsum(
        "rght,rtgd->rghd",
        weights.astype(jnp.bfloat16),
        kv_cache[..., head_size:],
        preferred_element_type=jnp.float32,
    )
    mixture = (
        mixture
        + own_low[..., None] * fresh_key_value[..., head_size:].astype(jnp.float32)[:, :, None, :]
    )
    return (mixture / denominator[..., None]).astype(jnp.bfloat16).reshape(count_req, -1)


def token_rows(hidden, routes, gates, experts):
    combine = gates / jnp.sum(gates, axis=1, keepdims=True)
    named = routes[:, :, None] == jnp.arange(experts, dtype=jnp.int32)[None, None, :]
    share = jnp.sum(jnp.where(named, combine[:, :, None], 0.0), axis=1)
    terms = []
    for _ in range(3):
        term = lax.reduce_precision(share, 8, 7)
        terms.append(term.astype(jnp.bfloat16))
        share = share - term
    fill = jnp.zeros((hidden.shape[0], EXTRA - 3 * experts), jnp.bfloat16)
    return jnp.concatenate([hidden, *terms, fill], axis=1)


def expert_kernel(pieces, inner, *refs):
    pick = refs[0]
    rows_in = refs[1 : 1 + len(pieces)]
    gate_own, up_own, gate_other, up_other, down_own, down_other = refs[1 + len(pieces) : 7 + len(pieces)]
    outs = refs[7 + len(pieces) : -3]
    rows, act, share = refs[-3:]
    width = gate_own.shape[0]
    block = gate_own.shape[1]
    steps = inner // block
    step = pl.program_id(0)

    @pl.when(step == 0)
    def _():
        start = 0
        for ref, (first, size) in zip(rows_in, pieces):
            taken = slice(first, first + size)
            rows[start : start + size, :] = ref[taken, :width]
            share[start : start + size, :] = jnp.sum(
                ref[taken, width:].astype(jnp.float32) * pick[...], axis=1, keepdims=True
            )
            start += size

    def hidden_block(gate, up):
        left = jnp.dot(rows[...], gate[...], preferred_element_type=jnp.float32)
        right = jnp.dot(rows[...], up[...], preferred_element_type=jnp.float32)
        act[:, pl.ds(pl.multiple_of(step * block, block), block)] = (jax.nn.silu(left) * right).astype(
            jnp.bfloat16
        )

    @pl.when(step < steps)
    def _():
        hidden_block(gate_own, up_own)

    @pl.when((step >= steps) & (step < 2 * steps))
    def _():
        hidden_block(gate_other, up_other)

    @pl.when(step >= 2 * steps)
    def _():
        total = jnp.dot(act[:, :inner], down_own[...], preferred_element_type=jnp.float32)
        total += jnp.dot(act[:, inner:], down_other[...], preferred_element_type=jnp.float32)
        total = (total * share[...]).astype(jnp.bfloat16)
        start = 0
        for out in outs:
            out[...] = total[start : start + out.shape[0], :]
            start += out.shape[0]


def experts_on(parts, sizes, pick, weights):
    (gate_up, down), (gate_up_other, down_other) = weights
    width, inner = gate_up.shape[0], down.shape[0]
    block, columns = 256, 512
    steps = inner // block
    count = sum(sizes)
    pieces = [piece for piece, _, _ in parts]
    taken = tuple((first, size) for _, first, size in parts)

    def part(first, offset):
        return pl.BlockSpec(
            (width, block), lambda i: (0, offset + jnp.clip(i - first, 0, steps - 1))
        )

    def column(i):
        return (0, jnp.maximum(i - 2 * steps, 0))

    whole = pl.BlockSpec(memory_space=pltpu.VMEM)
    held = (gate_up, gate_up, gate_up_other, gate_up_other, down, down_other)
    return pl.pallas_call(
        functools.partial(expert_kernel, taken, inner),
        grid=(2 * steps + width // columns,),
        in_specs=[whole] * (1 + len(pieces))
        + [part(0, 0), part(0, steps), part(steps, 0), part(steps, steps)]
        + [pl.BlockSpec((inner, columns), column)] * 2,
        out_specs=[pl.BlockSpec((size, columns), column) for size in sizes],
        out_shape=[jax.ShapeDtypeStruct((size, width), jnp.bfloat16) for size in sizes],
        scratch_shapes=[
            pltpu.VMEM((count, width), jnp.bfloat16),
            pltpu.VMEM((count, 2 * inner), jnp.bfloat16),
            pltpu.VMEM((count, 1), jnp.float32),
        ],
        compiler_params=pltpu.CompilerParams(vmem_limit_bytes=40 << 20),
        cost_estimate=pl.CostEstimate(
            flops=12 * count * width * inner,
            bytes_accessed=12 * width * inner + 4 * count * width,
            transcendentals=2 * count * inner,
        ),
    )(pick, *pieces, *(pltpu.with_memory_space_constraint(w, pltpu.HBM) for w in held))


def per_device(
    query, fresh_key_value, kv_cache, cache_lengths, hidden, routes, gates, w_gate_up, w_down
):
    sections = lax.axis_size("sec")
    section = lax.axis_index("sec")
    experts = lax.axis_size("dev") // 2
    expert = lax.axis_index("dev") // 2
    expert_side = section == sections - 1
    count = hidden.shape[0]
    f32 = jnp.float32

    gate_up, down = w_gate_up[0], w_down[0]
    weights = ((gate_up, down), (other_core(gate_up), other_core(down)))

    packed = token_rows(hidden, routes, gates, experts)
    block = jnp.concatenate([to_section(packed, s, sections - 1) for s in range(sections - 1)], axis=0)

    group = stacked([block, step_u(block, 1), step_u(block, -1), step_u(block, 2)])
    size = group.shape[0]
    cut = 16 * ((size // 2 + 15) // 16)
    before, after = step_v(group, 1), step_v(group, -1)
    across_a, across_b = step_v(before[:cut], 1), step_v(after[cut:], -1)

    attention_out = attention_block(query, fresh_key_value, kv_cache, cache_lengths)
    attention_out = jnp.where(expert_side, jnp.zeros_like(attention_out), attention_out)

    column = lax.broadcasted_iota(jnp.int32, (1, EXTRA), 1)
    pick = ((column % experts == expert) & (column < 3 * experts)).astype(f32)
    rest = size - cut
    cross_a, cross_b, after_b, before_a = experts_on(
        [(across_a, 0, cut), (across_b, 0, rest), (after, cut, rest), (before, 0, cut)],
        (cut, rest, rest, cut),
        pick,
        weights,
    )
    own_a, own_b, after_a, before_b = experts_on(
        [(group, 0, size), (after, 0, cut), (before, cut, rest)], (cut, rest, cut, rest), pick, weights
    )

    from_cross_a, from_cross_b = step_v(cross_a, 1), step_v(cross_b, -1)
    from_after_b, from_before_a = step_v(after_b, 1), step_v(before_a, -1)
    from_after_a = step_v((after_a.astype(f32) + from_cross_a.astype(f32)).astype(jnp.bfloat16), 1)
    from_before_b = step_v((before_b.astype(f32) + from_cross_b.astype(f32)).astype(jnp.bfloat16), -1)
    sum_a = own_a.astype(f32) + from_after_a.astype(f32) + from_before_a.astype(f32)
    sum_b = own_b.astype(f32) + from_after_b.astype(f32) + from_before_b.astype(f32)
    held = size // SIDE
    summed = jnp.concatenate([sum_a, sum_b], axis=0)
    low = summed.astype(jnp.bfloat16)
    total = (
        summed[:held]
        + step_u(low[held : 2 * held], -1).astype(f32)
        + step_u(low[2 * held : 3 * held], 1).astype(f32)
        + step_u(low[3 * held :], 2).astype(f32)
    ).astype(jnp.bfloat16)

    result = None
    for s in range(sections - 1):
        back = to_section(total[s * count : (s + 1) * count], sections - 1, s)
        result = back if result is None else result + back
    return attention_out, result


def solution(mesh):
    return jax.shard_map(
        per_device,
        mesh=mesh,
        in_specs=(
            P(("sec", "dev"), None),
            P(("sec", "dev"), None, None),
            P(("sec", "dev"), None, None, None),
            P(("sec", "dev")),
            P(("sec", "dev"), None),
            P(("sec", "dev"), None),
            P(("sec", "dev"), None),
            P(("sec", "dev"), None, None),
            P(("sec", "dev"), None, None),
        ),
        out_specs=(P(("sec", "dev"), None), P(("sec", "dev"), None)),
        check_vma=False,
    )
```

```python
import functools

import jax
import jax.numpy as jnp
from jax import lax
from jax.experimental import pallas as pl
from jax.experimental.pallas import tpu as pltpu
from jax.sharding import PartitionSpec as P

SIDE = 4
EXTRA = 128
VMEM_LIMIT = 6 << 20


def along(first, distance):
    pairs = []
    for i in range(2 * SIDE * SIDE):
        z, x, core = i // (2 * SIDE), i // 2 % SIDE, i % 2
        if first == (core == 0):
            x = (x + distance) % SIDE
        else:
            z = (z + distance) % SIDE
        pairs.append((i, (z * SIDE + x) * 2 + core))
    return pairs


def step_u(block, distance):
    return lax.ppermute(block, "dev", along(True, distance))


def step_v(block, distance):
    return lax.ppermute(block, "dev", along(False, distance))


def to_section(block, source, target):
    return lax.ppermute(block, "sec", [(source, target)])


def stacked(blocks):
    rows = sum(block.shape[0] for block in blocks)
    start, total = 0, None
    for block in blocks:
        size = block.shape[0]
        padded = jnp.pad(block, ((start, rows - start - size), (0, 0)))
        total = padded if total is None else total + padded
        start += size
    return total


def other_core(block):
    return lax.ppermute(block, "dev", [(i, i ^ 1) for i in range(2 * SIDE * SIDE)])


def attention_block(query, fresh_key_value, kv_cache, cache_lengths):
    count_req = query.shape[0]
    heads_kv = fresh_key_value.shape[1]
    head_size = fresh_key_value.shape[2] // 2
    group_size = query.shape[1] // (heads_kv * head_size)
    query_heads = query.reshape(count_req, heads_kv, group_size, head_size)
    score_scale = head_size ** (-0.5)
    scores = (
        jnp.einsum(
            "rghd,rtgd->rght",
            query_heads,
            kv_cache[..., :head_size],
            preferred_element_type=jnp.float32,
        )
        * score_scale
    )
    valid = jnp.arange(kv_cache.shape[1], dtype=jnp.int32)[None, :] < cache_lengths[:, None]
    scores = jnp.where(valid[:, None, None, :], scores, -jnp.inf)
    own_score = (
        jnp.einsum(
            "rghd,rgd->rgh",
            query_heads,
            fresh_key_value[..., :head_size],
            preferred_element_type=jnp.float32,
        )
        * score_scale
    )
    peak = jnp.maximum(jnp.max(scores, axis=-1), own_score)
    weights = jnp.exp(scores - peak[..., None])
    own_weight = jnp.exp(own_score - peak)
    denominator = jnp.sum(weights, axis=-1) + own_weight
    own_low = lax.optimization_barrier(own_weight.astype(jnp.bfloat16)).astype(jnp.float32)
    mixture = jnp.einsum(
        "rght,rtgd->rghd",
        weights.astype(jnp.bfloat16),
        kv_cache[..., head_size:],
        preferred_element_type=jnp.float32,
    )
    mixture = (
        mixture
        + own_low[..., None] * fresh_key_value[..., head_size:].astype(jnp.float32)[:, :, None, :]
    )
    return (mixture / denominator[..., None]).astype(jnp.bfloat16).reshape(count_req, -1)


def token_rows(hidden, routes, gates, experts):
    combine = gates / jnp.sum(gates, axis=1, keepdims=True)
    named = routes[:, :, None] == jnp.arange(experts, dtype=jnp.int32)[None, None, :]
    share = jnp.sum(jnp.where(named, combine[:, :, None], 0.0), axis=1)
    terms = []
    for _ in range(3):
        term = lax.reduce_precision(share, 8, 7)
        terms.append(term.astype(jnp.bfloat16))
        share = share - term
    fill = jnp.zeros((hidden.shape[0], EXTRA - 3 * experts), jnp.bfloat16)
    return jnp.concatenate([hidden, *terms, fill], axis=1)


def expert_kernel(parts, outputs, columns, load, *refs):
    refs = list(refs)
    pick = refs.pop(0)
    rows_in = [refs.pop(0) for _ in parts]
    weights = [refs.pop(0) for _ in range(4 if load else 6)]
    outs = [refs.pop(0) for _ in range(outputs)]
    copies = []
    if load:
        (gate_up, down, gate_up_other, down_other), weights = weights, [refs.pop(0) for _ in range(6)]
        sems = refs.pop()
        sources = []
        for both in (gate_up, gate_up_other):
            inner = both.shape[1] // 2
            sources += [both.at[:, :inner], both.at[:, inner:]]
        sources += [down, down_other]
        for i, (source, kept) in enumerate(zip(sources, weights)):
            copies.append(pltpu.make_async_copy(source, kept, sems.at[i]))
            copies[-1].start()
    rows, act, share = refs
    gate_ups, (down_own, down_other) = (weights[:2], weights[2:4]), weights[4:]
    inner, width = down_own.shape

    def arrived(index):
        if load:
            copies[index].wait()

    start = 0
    for ref, (first, size) in zip(rows_in, parts):
        taken = slice(first, first + size)
        rows[start : start + size, :] = ref[taken, :width]
        share[start : start + size, :] = jnp.sum(
            ref[taken, width:].astype(jnp.float32) * pick[...], axis=1, keepdims=True
        )
        start += size

    for half, (gate, up) in enumerate(gate_ups):
        arrived(2 * half)
        left = jnp.dot(rows[...], gate[...], preferred_element_type=jnp.float32)
        arrived(2 * half + 1)
        right = jnp.dot(rows[...], up[...], preferred_element_type=jnp.float32)
        act[:, half * inner : (half + 1) * inner] = (jax.nn.silu(left) * right).astype(jnp.bfloat16)
    arrived(4)
    arrived(5)

    @pl.loop(0, width // columns)
    def _(n):
        at = pl.ds(pl.multiple_of(n * columns, columns), columns)
        total = jnp.dot(act[:, :inner], down_own[:, at], preferred_element_type=jnp.float32)
        total += jnp.dot(act[:, inner:], down_other[:, at], preferred_element_type=jnp.float32)
        total = (total * share[...]).astype(jnp.bfloat16)
        start = 0
        for out in outs:
            out[:, at] = total[start : start + out.shape[0], :]
            start += out.shape[0]


def experts_on(parts, sizes, pick, weights, load=False):
    inner, width = weights[-1].shape
    count = sum(sizes)
    pieces = [piece for piece, _, _ in parts]
    taken = tuple((first, size) for _, first, size in parts)
    space = pltpu.HBM if load else pltpu.VMEM
    held = [pltpu.with_memory_space_constraint(w, space) for w in weights]
    whole = pl.BlockSpec(memory_space=pltpu.VMEM)
    there = pl.BlockSpec(memory_space=pl.ANY) if load else whole
    kept = [(width, inner)] * 4 + [(inner, width)] * 2 if load else []
    kept = [pltpu.VMEM(shape, jnp.bfloat16) for shape in kept]
    outs = pl.pallas_call(
        functools.partial(expert_kernel, taken, len(sizes), 1024, load),
        in_specs=[whole] * (1 + len(pieces)) + [there] * len(weights),
        out_specs=[whole] * (len(sizes) + len(kept)),
        out_shape=[jax.ShapeDtypeStruct((size, width), jnp.bfloat16) for size in sizes] + kept,
        scratch_shapes=[
            pltpu.VMEM((count, width), jnp.bfloat16),
            pltpu.VMEM((count, 2 * inner), jnp.bfloat16),
            pltpu.VMEM((count, 1), jnp.float32),
        ]
        + ([pltpu.SemaphoreType.DMA((6,))] if load else []),
        compiler_params=pltpu.CompilerParams(vmem_limit_bytes=VMEM_LIMIT),
        cost_estimate=pl.CostEstimate(
            flops=12 * count * width * inner,
            bytes_accessed=12 * width * inner if load else 4 * count * width,
            transcendentals=2 * count * inner,
        ),
    )(pick, *pieces, *held)
    return outs[: len(sizes)], outs[len(sizes) :]


def per_device(
    query, fresh_key_value, kv_cache, cache_lengths, hidden, routes, gates, w_gate_up, w_down
):
    sections = lax.axis_size("sec")
    section = lax.axis_index("sec")
    experts = lax.axis_size("dev") // 2
    expert = lax.axis_index("dev") // 2
    expert_side = section == sections - 1
    count = hidden.shape[0]
    f32 = jnp.float32

    gate_up, down = w_gate_up[0], w_down[0]
    weights = (gate_up, down, other_core(gate_up), other_core(down))

    packed = token_rows(hidden, routes, gates, experts)
    block = jnp.concatenate([to_section(packed, s, sections - 1) for s in range(sections - 1)], axis=0)

    group = stacked([block, step_u(block, 1), step_u(block, -1), step_u(block, 2)])
    size = group.shape[0]
    cut = 16 * ((size // 2 + 15) // 16)
    rest = size - cut
    before, after = step_v(group, 1), step_v(group, -1)
    column = lax.broadcasted_iota(jnp.int32, (1, EXTRA), 1)
    pick = ((column % experts == expert) & (column < 3 * experts)).astype(f32)
    (own_a, own_b), kept = experts_on([(group, 0, size)], (cut, rest), pick, weights, load=True)

    before, after, own_a, own_b = lax.optimization_barrier((before, after, own_a, own_b))
    across_a, across_b = step_v(before[:cut], 1), step_v(after[cut:], -1)
    (after_a, after_b, before_a, before_b), _ = experts_on(
        [(after, 0, size), (before, 0, size)], (cut, rest, cut, rest), pick, kept
    )
    across_a, across_b, after_a, after_b, before_a, before_b = lax.optimization_barrier(
        (across_a, across_b, after_a, after_b, before_a, before_b)
    )
    (cross_a, cross_b), _ = experts_on([(across_a, 0, cut), (across_b, 0, rest)], (cut, rest), pick, kept)

    attention_out = attention_block(query, fresh_key_value, kv_cache, cache_lengths)
    attention_out = jnp.where(expert_side, jnp.zeros_like(attention_out), attention_out)

    from_cross_a, from_cross_b = step_v(cross_a, 1), step_v(cross_b, -1)
    from_after_b, from_before_a = step_v(after_b, 1), step_v(before_a, -1)
    from_after_a = step_v((after_a.astype(f32) + from_cross_a.astype(f32)).astype(jnp.bfloat16), 1)
    from_before_b = step_v((before_b.astype(f32) + from_cross_b.astype(f32)).astype(jnp.bfloat16), -1)
    sum_a = own_a.astype(f32) + from_after_a.astype(f32) + from_before_a.astype(f32)
    sum_b = own_b.astype(f32) + from_after_b.astype(f32) + from_before_b.astype(f32)
    held = size // SIDE
    summed = jnp.concatenate([sum_a, sum_b], axis=0)
    low = summed.astype(jnp.bfloat16)
    total = (
        summed[:held]
        + step_u(low[held : 2 * held], -1).astype(f32)
        + step_u(low[2 * held : 3 * held], 1).astype(f32)
        + step_u(low[3 * held :], 2).astype(f32)
    ).astype(jnp.bfloat16)

    result = None
    for s in range(sections - 1):
        back = to_section(total[s * count : (s + 1) * count], sections - 1, s)
        result = back if result is None else result + back
    return attention_out, result


def solution(mesh):
    return jax.shard_map(
        per_device,
        mesh=mesh,
        in_specs=(
            P(("sec", "dev"), None),
            P(("sec", "dev"), None, None),
            P(("sec", "dev"), None, None, None),
            P(("sec", "dev")),
            P(("sec", "dev"), None),
            P(("sec", "dev"), None),
            P(("sec", "dev"), None),
            P(("sec", "dev"), None, None),
            P(("sec", "dev"), None, None),
        ),
        out_specs=(P(("sec", "dev"), None), P(("sec", "dev"), None)),
        check_vma=False,
    )
```

```python
import functools

import jax
import jax.numpy as jnp
from jax import lax
from jax.experimental import pallas as pl
from jax.experimental.pallas import tpu as pltpu
from jax.sharding import PartitionSpec as P

SIDE = 4
EXTRA = 128
VMEM_LIMIT = 6 << 20


def along(first, distance):
    pairs = []
    for i in range(2 * SIDE * SIDE):
        z, x, core = i // (2 * SIDE), i // 2 % SIDE, i % 2
        if first == (core == 0):
            x = (x + distance) % SIDE
        else:
            z = (z + distance) % SIDE
        pairs.append((i, (z * SIDE + x) * 2 + core))
    return pairs


def step_u(block, distance):
    return lax.ppermute(block, "dev", along(True, distance))


def step_v(block, distance):
    return lax.ppermute(block, "dev", along(False, distance))


def to_section(block, source, target):
    return lax.ppermute(block, "sec", [(source, target)])


def stacked(blocks):
    rows = sum(block.shape[0] for block in blocks)
    start, total = 0, None
    for block in blocks:
        size = block.shape[0]
        padded = jnp.pad(block, ((start, rows - start - size), (0, 0)))
        total = padded if total is None else total + padded
        start += size
    return total


def other_core(block):
    return lax.ppermute(block, "dev", [(i, i ^ 1) for i in range(2 * SIDE * SIDE)])


def attention_block(query, fresh_key_value, kv_cache, cache_lengths):
    count_req = query.shape[0]
    heads_kv = fresh_key_value.shape[1]
    head_size = fresh_key_value.shape[2] // 2
    group_size = query.shape[1] // (heads_kv * head_size)
    query_heads = query.reshape(count_req, heads_kv, group_size, head_size)
    score_scale = head_size ** (-0.5)
    scores = (
        jnp.einsum(
            "rghd,rtgd->rght",
            query_heads,
            kv_cache[..., :head_size],
            preferred_element_type=jnp.float32,
        )
        * score_scale
    )
    valid = jnp.arange(kv_cache.shape[1], dtype=jnp.int32)[None, :] < cache_lengths[:, None]
    scores = jnp.where(valid[:, None, None, :], scores, -jnp.inf)
    own_score = (
        jnp.einsum(
            "rghd,rgd->rgh",
            query_heads,
            fresh_key_value[..., :head_size],
            preferred_element_type=jnp.float32,
        )
        * score_scale
    )
    peak = jnp.maximum(jnp.max(scores, axis=-1), own_score)
    weights = jnp.exp(scores - peak[..., None])
    own_weight = jnp.exp(own_score - peak)
    denominator = jnp.sum(weights, axis=-1) + own_weight
    own_low = lax.optimization_barrier(own_weight.astype(jnp.bfloat16)).astype(jnp.float32)
    mixture = jnp.einsum(
        "rght,rtgd->rghd",
        weights.astype(jnp.bfloat16),
        kv_cache[..., head_size:],
        preferred_element_type=jnp.float32,
    )
    mixture = (
        mixture
        + own_low[..., None] * fresh_key_value[..., head_size:].astype(jnp.float32)[:, :, None, :]
    )
    return (mixture / denominator[..., None]).astype(jnp.bfloat16).reshape(count_req, -1)


def pack_kernel(experts, hidden, routes, gates, out):
    count, width = hidden.shape
    out[:, :width] = hidden[...]
    combine = gates[...] / jnp.sum(gates[...], axis=0, keepdims=True)
    place = lax.broadcasted_iota(jnp.int32, (EXTRA, count), 0)
    share = jnp.zeros((EXTRA, count), jnp.float32)
    for k in range(routes.shape[0]):
        named = routes[k : k + 1, :] == place % experts
        share += jnp.where(named, combine[k : k + 1, :], 0.0)
    terms = []
    for _ in range(3):
        terms.append(share.astype(jnp.bfloat16).astype(jnp.float32))
        share = share - terms[-1]
    packed = jnp.where(place < experts, terms[0], jnp.where(place < 2 * experts, terms[1], terms[2]))
    packed = jnp.where(place < 3 * experts, packed, 0.0).astype(jnp.bfloat16)
    same = lax.broadcasted_iota(jnp.int32, (count, count), 0) == lax.broadcasted_iota(
        jnp.int32, (count, count), 1
    )
    turned = lax.dot_general(
        same.astype(jnp.float32).astype(jnp.bfloat16),
        packed,
        (((1,), (1,)), ((), ())),
        preferred_element_type=jnp.float32,
    )
    out[:, width:] = turned.astype(jnp.bfloat16)


def token_rows(hidden, routes, gates, experts):
    count, width = hidden.shape
    whole = pl.BlockSpec(memory_space=pltpu.VMEM)
    return pl.pallas_call(
        functools.partial(pack_kernel, experts),
        in_specs=[whole] * 3,
        out_specs=whole,
        out_shape=jax.ShapeDtypeStruct((count, width + EXTRA), hidden.dtype),
        compiler_params=pltpu.CompilerParams(vmem_limit_bytes=VMEM_LIMIT),
    )(hidden, routes.T, gates.T)


def expert_kernel(parts, outputs, columns, load, *refs):
    refs = list(refs)
    pick = refs.pop(0)
    rows_in = [refs.pop(0) for _ in parts]
    weights = [refs.pop(0) for _ in range(4 if load else 6)]
    outs = [refs.pop(0) for _ in range(outputs)]
    copies = []
    if load:
        (gate_up, down, gate_up_other, down_other), weights = weights, [refs.pop(0) for _ in range(6)]
        sems = refs.pop()
        sources = []
        for both in (gate_up, gate_up_other):
            inner = both.shape[1] // 2
            sources += [both.at[:, :inner], both.at[:, inner:]]
        sources += [down, down_other]
        for i, (source, kept) in enumerate(zip(sources, weights)):
            copies.append(pltpu.make_async_copy(source, kept, sems.at[i]))
            copies[-1].start()
    rows, act, share = refs
    gate_ups, (down_own, down_other) = (weights[:2], weights[2:4]), weights[4:]
    inner, width = down_own.shape

    def arrived(index):
        if load:
            copies[index].wait()

    start = 0
    for ref, (first, size) in zip(rows_in, parts):
        taken = slice(first, first + size)
        rows[start : start + size, :] = ref[taken, :width]
        share[start : start + size, :] = jnp.sum(
            ref[taken, width:].astype(jnp.float32) * pick[...], axis=1, keepdims=True
        )
        start += size

    for half, (gate, up) in enumerate(gate_ups):
        arrived(2 * half)
        left = jnp.dot(rows[...], gate[...], preferred_element_type=jnp.float32)
        arrived(2 * half + 1)
        right = jnp.dot(rows[...], up[...], preferred_element_type=jnp.float32)
        act[:, half * inner : (half + 1) * inner] = (jax.nn.silu(left) * right).astype(jnp.bfloat16)
    arrived(4)
    arrived(5)

    @pl.loop(0, width // columns)
    def _(n):
        at = pl.ds(pl.multiple_of(n * columns, columns), columns)
        total = jnp.dot(act[:, :inner], down_own[:, at], preferred_element_type=jnp.float32)
        total += jnp.dot(act[:, inner:], down_other[:, at], preferred_element_type=jnp.float32)
        total = (total * share[...]).astype(jnp.bfloat16)
        start = 0
        for out in outs:
            out[:, at] = total[start : start + out.shape[0], :]
            start += out.shape[0]


def experts_on(parts, sizes, pick, weights, load=False):
    inner, width = weights[-1].shape
    count = sum(sizes)
    pieces = [piece for piece, _, _ in parts]
    taken = tuple((first, size) for _, first, size in parts)
    space = pltpu.HBM if load else pltpu.VMEM
    held = [pltpu.with_memory_space_constraint(w, space) for w in weights]
    whole = pl.BlockSpec(memory_space=pltpu.VMEM)
    there = pl.BlockSpec(memory_space=pl.ANY) if load else whole
    kept = [(width, inner)] * 4 + [(inner, width)] * 2 if load else []
    kept = [pltpu.VMEM(shape, jnp.bfloat16) for shape in kept]
    outs = pl.pallas_call(
        functools.partial(expert_kernel, taken, len(sizes), 1024, load),
        in_specs=[whole] * (1 + len(pieces)) + [there] * len(weights),
        out_specs=[whole] * (len(sizes) + len(kept)),
        out_shape=[jax.ShapeDtypeStruct((size, width), jnp.bfloat16) for size in sizes] + kept,
        scratch_shapes=[
            pltpu.VMEM((count, width), jnp.bfloat16),
            pltpu.VMEM((count, 2 * inner), jnp.bfloat16),
            pltpu.VMEM((count, 1), jnp.float32),
        ]
        + ([pltpu.SemaphoreType.DMA((6,))] if load else []),
        compiler_params=pltpu.CompilerParams(vmem_limit_bytes=VMEM_LIMIT),
        cost_estimate=pl.CostEstimate(
            flops=12 * count * width * inner,
            bytes_accessed=12 * width * inner if load else 4 * count * width,
            transcendentals=2 * count * inner,
        ),
    )(pick, *pieces, *held)
    return outs[: len(sizes)], outs[len(sizes) :]


def per_device(
    query, fresh_key_value, kv_cache, cache_lengths, hidden, routes, gates, w_gate_up, w_down
):
    sections = lax.axis_size("sec")
    section = lax.axis_index("sec")
    experts = lax.axis_size("dev") // 2
    expert = lax.axis_index("dev") // 2
    expert_side = section == sections - 1
    count = hidden.shape[0]
    f32 = jnp.float32

    gate_up, down = w_gate_up[0], w_down[0]
    weights = (gate_up, down, other_core(gate_up), other_core(down))

    packed = token_rows(hidden, routes, gates, experts)
    block = jnp.concatenate([to_section(packed, s, sections - 1) for s in range(sections - 1)], axis=0)

    group = stacked([block, step_u(block, 1), step_u(block, -1), step_u(block, 2)])
    size = group.shape[0]
    cut = 16 * ((size // 2 + 15) // 16)
    rest = size - cut
    before, after = step_v(group, 1), step_v(group, -1)
    column = lax.broadcasted_iota(jnp.int32, (1, EXTRA), 1)
    pick = ((column % experts == expert) & (column < 3 * experts)).astype(f32)
    (own_a, own_b), kept = experts_on([(group, 0, size)], (cut, rest), pick, weights, load=True)

    before, after, own_a, own_b = lax.optimization_barrier((before, after, own_a, own_b))
    across_a, across_b = step_v(before[:cut], 1), step_v(after[cut:], -1)
    (after_a, after_b, before_a, before_b), _ = experts_on(
        [(after, 0, size), (before, 0, size)], (cut, rest, cut, rest), pick, kept
    )
    across_a, across_b, after_a, after_b, before_a, before_b = lax.optimization_barrier(
        (across_a, across_b, after_a, after_b, before_a, before_b)
    )
    from_after_b, from_before_a = step_v(after_b, 1), step_v(before_a, -1)
    (cross_a, cross_b), _ = experts_on([(across_a, 0, cut), (across_b, 0, rest)], (cut, rest), pick, kept)
    from_after_b, from_before_a, cross_a, cross_b = lax.optimization_barrier(
        (from_after_b, from_before_a, cross_a, cross_b)
    )
    from_cross_a, from_cross_b = step_v(cross_a, 1), step_v(cross_b, -1)

    query, _ = lax.optimization_barrier((query, cross_a))
    attention_out = lax.cond(
        expert_side,
        lambda query, *_: jnp.zeros_like(query),
        attention_block,
        query,
        fresh_key_value,
        kv_cache,
        cache_lengths,
    )

    from_before_b = step_v((before_b.astype(f32) + from_cross_b.astype(f32)).astype(jnp.bfloat16), -1)
    from_after_a = step_v((after_a.astype(f32) + from_cross_a.astype(f32)).astype(jnp.bfloat16), 1)
    held = size // SIDE
    near = 2 * held - (cut - held)
    sum_b = own_b.astype(f32) + from_after_b.astype(f32) + from_before_b.astype(f32)
    far = sum_b[near:].astype(jnp.bfloat16)
    part = held // 2
    from_far_a, from_far_b = step_u(far[:part], 1), step_u(far[part:], -1)
    sum_a = own_a.astype(f32) + from_after_a.astype(f32) + from_before_a.astype(f32)
    ahead = jnp.concatenate([sum_a[2 * held :], sum_b[:near]], axis=0)
    ahead = ahead + jnp.pad(from_far_a.astype(f32), ((0, held - part), (0, 0)))
    behind = sum_a[held : 2 * held] + jnp.pad(from_far_b.astype(f32), ((part, 0), (0, 0)))
    total = (
        sum_a[:held]
        + step_u(ahead.astype(jnp.bfloat16), 1).astype(f32)
        + step_u(behind.astype(jnp.bfloat16), -1).astype(f32)
    ).astype(jnp.bfloat16)

    result = None
    for s in range(sections - 1):
        back = to_section(total[s * count : (s + 1) * count], sections - 1, s)
        result = back if result is None else result + back
    return attention_out, result


def solution(mesh):
    return jax.shard_map(
        per_device,
        mesh=mesh,
        in_specs=(
            P(("sec", "dev"), None),
            P(("sec", "dev"), None, None),
            P(("sec", "dev"), None, None, None),
            P(("sec", "dev")),
            P(("sec", "dev"), None),
            P(("sec", "dev"), None),
            P(("sec", "dev"), None),
            P(("sec", "dev"), None, None),
            P(("sec", "dev"), None, None),
        ),
        out_specs=(P(("sec", "dev"), None), P(("sec", "dev"), None)),
        check_vma=False,
    )
```

```python
import functools

import jax
import jax.numpy as jnp
from jax import lax
from jax.experimental import pallas as pl
from jax.experimental.pallas import tpu as pltpu
from jax.sharding import PartitionSpec as P

SIDE = 4
EXTRA = 128
VMEM_LIMIT = 6 << 20


def along(first, distance):
    pairs = []
    for i in range(2 * SIDE * SIDE):
        z, x, core = i // (2 * SIDE), i // 2 % SIDE, i % 2
        if first == (core == 0):
            x = (x + distance) % SIDE
        else:
            z = (z + distance) % SIDE
        pairs.append((i, (z * SIDE + x) * 2 + core))
    return pairs


def step_u(block, distance):
    return lax.ppermute(block, "dev", along(True, distance))


def step_v(block, distance):
    return lax.ppermute(block, "dev", along(False, distance))


def to_section(block, source, target):
    return lax.ppermute(block, "sec", [(source, target)])


def stacked(blocks):
    rows = sum(block.shape[0] for block in blocks)
    start, total = 0, None
    for block in blocks:
        size = block.shape[0]
        padded = jnp.pad(block, ((start, rows - start - size), (0, 0)))
        total = padded if total is None else total + padded
        start += size
    return total


def other_core(block):
    return lax.ppermute(block, "dev", [(i, i ^ 1) for i in range(2 * SIDE * SIDE)])


def attention_block(query, fresh_key_value, kv_cache, cache_lengths):
    count_req = query.shape[0]
    heads_kv = fresh_key_value.shape[1]
    head_size = fresh_key_value.shape[2] // 2
    group_size = query.shape[1] // (heads_kv * head_size)
    query_heads = query.reshape(count_req, heads_kv, group_size, head_size)
    score_scale = head_size ** (-0.5)
    scores = (
        jnp.einsum(
            "rghd,rtgd->rght",
            query_heads,
            kv_cache[..., :head_size],
            preferred_element_type=jnp.float32,
        )
        * score_scale
    )
    valid = jnp.arange(kv_cache.shape[1], dtype=jnp.int32)[None, :] < cache_lengths[:, None]
    scores = jnp.where(valid[:, None, None, :], scores, -jnp.inf)
    own_score = (
        jnp.einsum(
            "rghd,rgd->rgh",
            query_heads,
            fresh_key_value[..., :head_size],
            preferred_element_type=jnp.float32,
        )
        * score_scale
    )
    peak = jnp.maximum(jnp.max(scores, axis=-1), own_score)
    weights = jnp.exp(scores - peak[..., None])
    own_weight = jnp.exp(own_score - peak)
    denominator = jnp.sum(weights, axis=-1) + own_weight
    own_low = lax.optimization_barrier(own_weight.astype(jnp.bfloat16)).astype(jnp.float32)
    mixture = jnp.einsum(
        "rght,rtgd->rghd",
        weights.astype(jnp.bfloat16),
        kv_cache[..., head_size:],
        preferred_element_type=jnp.float32,
    )
    mixture = (
        mixture
        + own_low[..., None] * fresh_key_value[..., head_size:].astype(jnp.float32)[:, :, None, :]
    )
    return (mixture / denominator[..., None]).astype(jnp.bfloat16).reshape(count_req, -1)


def pack_kernel(experts, hidden, routes_in, gates_in, out, routes, gates, sems):
    count, width = hidden.shape
    pairs = ((routes_in, routes), (gates_in, gates), (hidden, out.at[:, :width]))
    copies = [pltpu.make_async_copy(*pair, sems.at[i]) for i, pair in enumerate(pairs)]
    for copy in copies:
        copy.start()
    copies[0].wait()
    copies[1].wait()
    combine = gates[...] / jnp.sum(gates[...], axis=0, keepdims=True)
    place = lax.broadcasted_iota(jnp.int32, (EXTRA, count), 0)
    share = jnp.zeros((EXTRA, count), jnp.float32)
    for k in range(routes.shape[0]):
        named = routes[k : k + 1, :] == place % experts
        share += jnp.where(named, combine[k : k + 1, :], 0.0)
    terms = []
    for _ in range(3):
        terms.append(share.astype(jnp.bfloat16).astype(jnp.float32))
        share = share - terms[-1]
    packed = jnp.where(place < experts, terms[0], jnp.where(place < 2 * experts, terms[1], terms[2]))
    packed = jnp.where(place < 3 * experts, packed, 0.0).astype(jnp.bfloat16)
    same = lax.broadcasted_iota(jnp.int32, (count, count), 0) == lax.broadcasted_iota(
        jnp.int32, (count, count), 1
    )
    turned = lax.dot_general(
        same.astype(jnp.float32).astype(jnp.bfloat16),
        packed,
        (((1,), (1,)), ((), ())),
        preferred_element_type=jnp.float32,
    )
    out[:, width:] = turned.astype(jnp.bfloat16)
    copies[2].wait()


def token_rows(hidden, routes, gates, experts):
    count, width = hidden.shape
    whole = pl.BlockSpec(memory_space=pltpu.VMEM)
    return pl.pallas_call(
        functools.partial(pack_kernel, experts),
        in_specs=[pl.BlockSpec(memory_space=pl.ANY)] * 3,
        out_specs=whole,
        out_shape=jax.ShapeDtypeStruct((count, width + EXTRA), hidden.dtype),
        scratch_shapes=[
            pltpu.VMEM(routes.shape[::-1], routes.dtype),
            pltpu.VMEM(gates.shape[::-1], gates.dtype),
            pltpu.SemaphoreType.DMA((3,)),
        ],
        compiler_params=pltpu.CompilerParams(vmem_limit_bytes=VMEM_LIMIT),
    )(*(pltpu.with_memory_space_constraint(w, pltpu.HBM) for w in (hidden, routes.T, gates.T)))


def weight_copies(gate_up, down, kept, sems):
    inner = down.shape[0]
    sources = (gate_up.at[:, :inner], gate_up.at[:, inner:], down)
    return [pltpu.make_async_copy(*pair, sems.at[i]) for i, pair in enumerate(zip(sources, kept))]


def kept_shapes(gate_up, down):
    inner, width = down.shape
    shapes = [(width, inner), (width, inner), (inner, width)]
    return [pltpu.VMEM(shape, down.dtype) for shape in shapes]


def expert_kernel(parts, outputs, columns, load, *refs):
    refs = list(refs)
    pick = refs.pop(0)
    rows_in = [refs.pop(0) for _ in parts]
    halves = [[refs.pop(0) for _ in range(2 if load else 3)] for _ in range(2)]
    outs = [refs.pop(0) for _ in range(outputs)]
    copies = []
    if load:
        kept = [[refs.pop(0) for _ in range(3)] for _ in range(2)]
        sems = refs.pop()
        for half in range(2):
            copies += weight_copies(*halves[half], kept[half], sems.at[half])
        halves = kept
        for index in (0, 1, 3, 4, 2, 5):
            copies[index].start()
    rows, act, share = refs
    inner, width = halves[0][2].shape

    def arrived(index):
        if load:
            copies[index].wait()

    start = 0
    for ref, (first, size) in zip(rows_in, parts):
        taken = slice(first, first + size)
        rows[start : start + size, :] = ref[taken, :width]
        share[start : start + size, :] = jnp.sum(
            ref[taken, width:].astype(jnp.float32) * pick[...], axis=1, keepdims=True
        )
        start += size

    for half, (gate, up, _) in enumerate(halves):
        arrived(3 * half)
        left = jnp.dot(rows[...], gate[...], preferred_element_type=jnp.float32)
        arrived(3 * half + 1)
        right = jnp.dot(rows[...], up[...], preferred_element_type=jnp.float32)
        act[:, half * inner : (half + 1) * inner] = (jax.nn.silu(left) * right).astype(jnp.bfloat16)
    arrived(2)
    arrived(5)

    @pl.loop(0, width // columns)
    def _(n):
        at = pl.ds(pl.multiple_of(n * columns, columns), columns)
        total = jnp.dot(act[:, :inner], halves[0][2][:, at], preferred_element_type=jnp.float32)
        total += jnp.dot(act[:, inner:], halves[1][2][:, at], preferred_element_type=jnp.float32)
        total = (total * share[...]).astype(jnp.bfloat16)
        start = 0
        for out in outs:
            out[:, at] = total[start : start + out.shape[0], :]
            start += out.shape[0]


def experts_on(parts, sizes, pick, halves):
    inner, width = halves[0][-1].shape
    load = len(halves[0]) == 2
    count = sum(sizes)
    pieces = [piece for piece, _, _ in parts]
    taken = tuple((first, size) for _, first, size in parts)
    whole = pl.BlockSpec(memory_space=pltpu.VMEM)
    space = pl.BlockSpec(memory_space=pl.ANY) if load else whole
    constraint = pltpu.HBM if load else pltpu.VMEM
    held = [pltpu.with_memory_space_constraint(w, constraint) for half in halves for w in half]
    kept = [shape for half in halves for shape in kept_shapes(*half)] if load else []
    outs = pl.pallas_call(
        functools.partial(expert_kernel, taken, len(sizes), 1024, load),
        in_specs=[whole] * (1 + len(pieces)) + [space] * len(held),
        out_specs=[whole] * (len(sizes) + len(kept)),
        out_shape=[jax.ShapeDtypeStruct((size, width), jnp.bfloat16) for size in sizes] + kept,
        scratch_shapes=[
            pltpu.VMEM((count, width), jnp.bfloat16),
            pltpu.VMEM((count, 2 * inner), jnp.bfloat16),
            pltpu.VMEM((count, 1), jnp.float32),
        ]
        + ([pltpu.SemaphoreType.DMA((2, 3))] if load else []),
        compiler_params=pltpu.CompilerParams(vmem_limit_bytes=VMEM_LIMIT),
        cost_estimate=pl.CostEstimate(
            flops=12 * count * width * inner,
            bytes_accessed=12 * width * inner if load else 4 * count * width,
            transcendentals=2 * count * inner,
        ),
    )(pick, *pieces, *held)
    kept = outs[len(sizes) :]
    return outs[: len(sizes)], (kept[:3], kept[3:]) if load else halves


def per_device(
    query, fresh_key_value, kv_cache, cache_lengths, hidden, routes, gates, w_gate_up, w_down
):
    sections = lax.axis_size("sec")
    section = lax.axis_index("sec")
    experts = lax.axis_size("dev") // 2
    expert = lax.axis_index("dev") // 2
    expert_side = section == sections - 1
    count = hidden.shape[0]
    f32 = jnp.float32

    gate_up, down = w_gate_up[0], w_down[0]
    halves = ((gate_up, down), (other_core(gate_up), other_core(down)))

    packed = token_rows(hidden, routes, gates, experts)
    blocks = [to_section(packed, s, sections - 1) for s in range(sections - 1)]
    block = jnp.concatenate(blocks, axis=0)

    group = stacked([block, step_u(block, 1), step_u(block, -1), step_u(block, 2)])
    size = group.shape[0]
    cut = 16 * ((size // 2 + 15) // 16)
    rest = size - cut
    before, after = step_v(group, 1), step_v(group, -1)
    column = lax.broadcasted_iota(jnp.int32, (1, EXTRA), 1)
    pick = ((column % experts == expert) & (column < 3 * experts)).astype(f32)
    (own_a, own_b), halves = experts_on([(group, 0, size)], (cut, rest), pick, halves)

    before, after, own_a, own_b = lax.optimization_barrier((before, after, own_a, own_b))
    across_a, across_b = step_v(before[:cut], 1), step_v(after[cut:], -1)
    (after_b, before_a), _ = experts_on([(after, cut, rest), (before, 0, cut)], (rest, cut), pick, halves)
    across_a, across_b, after_b, before_a = lax.optimization_barrier((across_a, across_b, after_b, before_a))

    from_after_b, from_before_a = step_v(after_b, 1), step_v(before_a, -1)
    (cross_a, cross_b), _ = experts_on(
        [(across_a, 0, cut), (across_b, 0, rest)], (cut, rest), pick, halves
    )
    from_cross_a, from_cross_b = step_v(cross_a, 1), step_v(cross_b, -1)
    after, before, from_after_b, from_before_a, cross_a = lax.optimization_barrier(
        (after, before, from_after_b, from_before_a, cross_a)
    )
    (after_a, before_b), _ = experts_on([(after, 0, cut), (before, cut, rest)], (cut, rest), pick, halves)

    query, _ = lax.optimization_barrier((query, cross_a))
    attention_out = lax.cond(
        expert_side,
        lambda query, *_: jnp.zeros_like(query),
        attention_block,
        query,
        fresh_key_value,
        kv_cache,
        cache_lengths,
    )

    from_before_b = step_v((before_b.astype(f32) + from_cross_b.astype(f32)).astype(jnp.bfloat16), -1)
    from_after_a = step_v((after_a.astype(f32) + from_cross_a.astype(f32)).astype(jnp.bfloat16), 1)
    held = size // SIDE
    near = 2 * held - (cut - held)
    sum_b = own_b.astype(f32) + from_after_b.astype(f32) + from_before_b.astype(f32)
    far = sum_b[near:].astype(jnp.bfloat16)
    part = held // 2
    from_far_a, from_far_b = step_u(far[:part], 1), step_u(far[part:], -1)
    sum_a = own_a.astype(f32) + from_after_a.astype(f32) + from_before_a.astype(f32)
    ahead = jnp.concatenate([sum_a[2 * held :], sum_b[:near]], axis=0)
    ahead = ahead + jnp.pad(from_far_a.astype(f32), ((0, held - part), (0, 0)))
    behind = sum_a[held : 2 * held] + jnp.pad(from_far_b.astype(f32), ((part, 0), (0, 0)))
    total = (
        sum_a[:held]
        + step_u(ahead.astype(jnp.bfloat16), 1).astype(f32)
        + step_u(behind.astype(jnp.bfloat16), -1).astype(f32)
    ).astype(jnp.bfloat16)

    result = None
    for s in range(sections - 1):
        back = to_section(total[s * count : (s + 1) * count], sections - 1, s)
        result = back if result is None else result + back
    return attention_out, result


def solution(mesh):
    return jax.shard_map(
        per_device,
        mesh=mesh,
        in_specs=(
            P(("sec", "dev"), None),
            P(("sec", "dev"), None, None),
            P(("sec", "dev"), None, None, None),
            P(("sec", "dev")),
            P(("sec", "dev"), None),
            P(("sec", "dev"), None),
            P(("sec", "dev"), None),
            P(("sec", "dev"), None, None),
            P(("sec", "dev"), None, None),
        ),
        out_specs=(P(("sec", "dev"), None), P(("sec", "dev"), None)),
        check_vma=False,
    )
```

```python
import functools

import jax
import jax.numpy as jnp
from jax import lax
from jax.experimental import pallas as pl
from jax.experimental.pallas import tpu as pltpu
from jax.sharding import PartitionSpec as P

SIDE = 4
EXTRA = 128
VMEM_LIMIT = 6 << 20


def along(first, distance):
    pairs = []
    for i in range(2 * SIDE * SIDE):
        z, x, core = i // (2 * SIDE), i // 2 % SIDE, i % 2
        if first == (core == 0):
            x = (x + distance) % SIDE
        else:
            z = (z + distance) % SIDE
        pairs.append((i, (z * SIDE + x) * 2 + core))
    return pairs


def step_u(block, distance):
    return lax.ppermute(block, "dev", along(True, distance))


def step_v(block, distance):
    return lax.ppermute(block, "dev", along(False, distance))


def to_section(block, source, target):
    return lax.ppermute(block, "sec", [(source, target)])


def stacked(blocks):
    rows = sum(block.shape[0] for block in blocks)
    start, total = 0, None
    for block in blocks:
        size = block.shape[0]
        padded = jnp.pad(block, ((start, rows - start - size), (0, 0)))
        total = padded if total is None else total + padded
        start += size
    return total


def other_core(block):
    return lax.ppermute(block, "dev", [(i, i ^ 1) for i in range(2 * SIDE * SIDE)])


def attention_block(query, fresh_key_value, kv_cache, cache_lengths):
    count_req = query.shape[0]
    heads_kv = fresh_key_value.shape[1]
    head_size = fresh_key_value.shape[2] // 2
    group_size = query.shape[1] // (heads_kv * head_size)
    query_heads = query.reshape(count_req, heads_kv, group_size, head_size)
    score_scale = head_size ** (-0.5)
    scores = (
        jnp.einsum(
            "rghd,rtgd->rght",
            query_heads,
            kv_cache[..., :head_size],
            preferred_element_type=jnp.float32,
        )
        * score_scale
    )
    valid = jnp.arange(kv_cache.shape[1], dtype=jnp.int32)[None, :] < cache_lengths[:, None]
    scores = jnp.where(valid[:, None, None, :], scores, -jnp.inf)
    own_score = (
        jnp.einsum(
            "rghd,rgd->rgh",
            query_heads,
            fresh_key_value[..., :head_size],
            preferred_element_type=jnp.float32,
        )
        * score_scale
    )
    peak = jnp.maximum(jnp.max(scores, axis=-1), own_score)
    weights = jnp.exp(scores - peak[..., None])
    own_weight = jnp.exp(own_score - peak)
    denominator = jnp.sum(weights, axis=-1) + own_weight
    own_low = lax.optimization_barrier(own_weight.astype(jnp.bfloat16)).astype(jnp.float32)
    mixture = jnp.einsum(
        "rght,rtgd->rghd",
        weights.astype(jnp.bfloat16),
        kv_cache[..., head_size:],
        preferred_element_type=jnp.float32,
    )
    mixture = (
        mixture
        + own_low[..., None] * fresh_key_value[..., head_size:].astype(jnp.float32)[:, :, None, :]
    )
    return (mixture / denominator[..., None]).astype(jnp.bfloat16).reshape(count_req, -1)


def pack_kernel(experts, hidden, routes_in, gates_in, out, routes, gates, sems):
    count, width = hidden.shape
    pairs = ((routes_in, routes), (gates_in, gates), (hidden, out.at[:, :width]))
    copies = [pltpu.make_async_copy(*pair, sems.at[i]) for i, pair in enumerate(pairs)]
    for copy in copies:
        copy.start()
    copies[0].wait()
    copies[1].wait()
    combine = gates[...] / jnp.sum(gates[...], axis=0, keepdims=True)
    place = lax.broadcasted_iota(jnp.int32, (EXTRA, count), 0)
    share = jnp.zeros((EXTRA, count), jnp.float32)
    for k in range(routes.shape[0]):
        named = routes[k : k + 1, :] == place % experts
        share += jnp.where(named, combine[k : k + 1, :], 0.0)
    terms = []
    for _ in range(3):
        terms.append(share.astype(jnp.bfloat16).astype(jnp.float32))
        share = share - terms[-1]
    packed = jnp.where(place < experts, terms[0], jnp.where(place < 2 * experts, terms[1], terms[2]))
    packed = jnp.where(place < 3 * experts, packed, 0.0).astype(jnp.bfloat16)
    same = lax.broadcasted_iota(jnp.int32, (count, count), 0) == lax.broadcasted_iota(
        jnp.int32, (count, count), 1
    )
    turned = lax.dot_general(
        same.astype(jnp.float32).astype(jnp.bfloat16),
        packed,
        (((1,), (1,)), ((), ())),
        preferred_element_type=jnp.float32,
    )
    out[:, width:] = turned.astype(jnp.bfloat16)
    copies[2].wait()


def token_rows(hidden, routes, gates, experts):
    count, width = hidden.shape
    whole = pl.BlockSpec(memory_space=pltpu.VMEM)
    return pl.pallas_call(
        functools.partial(pack_kernel, experts),
        in_specs=[pl.BlockSpec(memory_space=pl.ANY)] * 3,
        out_specs=whole,
        out_shape=jax.ShapeDtypeStruct((count, width + EXTRA), hidden.dtype),
        scratch_shapes=[
            pltpu.VMEM(routes.shape[::-1], routes.dtype),
            pltpu.VMEM(gates.shape[::-1], gates.dtype),
            pltpu.SemaphoreType.DMA((3,)),
        ],
        compiler_params=pltpu.CompilerParams(vmem_limit_bytes=VMEM_LIMIT),
    )(*(pltpu.with_memory_space_constraint(w, pltpu.HBM) for w in (hidden, routes.T, gates.T)))


def weight_copies(gate_up, down, kept, sems):
    inner = down.shape[0]
    sources = (gate_up.at[:, :inner], gate_up.at[:, inner:], down)
    return [pltpu.make_async_copy(*pair, sems.at[i]) for i, pair in enumerate(zip(sources, kept))]


def kept_shapes(gate_up, down):
    inner, width = down.shape
    shapes = [(width, inner), (width, inner), (inner, width)]
    return [pltpu.VMEM(shape, down.dtype) for shape in shapes]


def expert_kernel(pieces, columns, load, *refs):
    refs = list(refs)
    pick = refs.pop(0)
    rows_in = [refs.pop(0) for _ in range(pieces)]
    halves = [[refs.pop(0) for _ in range(2 if load else 3)] for _ in range(2)]
    outs = [refs.pop(0) for _ in range(pieces)]
    copies = []
    if load:
        kept = [[refs.pop(0) for _ in range(3)] for _ in range(2)]
        sems = refs.pop()
        for half in range(2):
            copies += weight_copies(*halves[half], kept[half], sems.at[half])
        halves = kept
        for index in (0, 1, 3, 4, 2, 5):
            copies[index].start()
    rows, act, share = refs
    inner, width = halves[0][2].shape

    def arrived(index):
        if load:
            copies[index].wait()

    start = 0
    for ref in rows_in:
        size = ref.shape[0]
        rows[start : start + size, :] = ref[:, :width]
        share[start : start + size, :] = jnp.sum(
            ref[:, width:].astype(jnp.float32) * pick[...], axis=1, keepdims=True
        )
        start += size

    for half, (gate, up, _) in enumerate(halves):
        arrived(3 * half)
        left = jnp.dot(rows[...], gate[...], preferred_element_type=jnp.float32)
        arrived(3 * half + 1)
        right = jnp.dot(rows[...], up[...], preferred_element_type=jnp.float32)
        act[:, half * inner : (half + 1) * inner] = (jax.nn.silu(left) * right).astype(jnp.bfloat16)
    arrived(2)
    arrived(5)

    @pl.loop(0, width // columns)
    def _(n):
        at = pl.ds(pl.multiple_of(n * columns, columns), columns)
        total = jnp.dot(act[:, :inner], halves[0][2][:, at], preferred_element_type=jnp.float32)
        total += jnp.dot(act[:, inner:], halves[1][2][:, at], preferred_element_type=jnp.float32)
        total = (total * share[...]).astype(jnp.bfloat16)
        start = 0
        for out in outs:
            out[:, at] = total[start : start + out.shape[0], :]
            start += out.shape[0]


def experts_on(pieces, pick, halves):
    inner, width = halves[0][-1].shape
    load = len(halves[0]) == 2
    sizes = [piece.shape[0] for piece in pieces]
    count = sum(sizes)
    whole = pl.BlockSpec(memory_space=pltpu.VMEM)
    space = pl.BlockSpec(memory_space=pl.ANY) if load else whole
    constraint = pltpu.HBM if load else pltpu.VMEM
    held = [pltpu.with_memory_space_constraint(w, constraint) for half in halves for w in half]
    kept = [shape for half in halves for shape in kept_shapes(*half)] if load else []
    outs = pl.pallas_call(
        functools.partial(expert_kernel, len(pieces), 1024, load),
        in_specs=[whole] * (1 + len(pieces)) + [space] * len(held),
        out_specs=[whole] * (len(sizes) + len(kept)),
        out_shape=[jax.ShapeDtypeStruct((size, width), jnp.bfloat16) for size in sizes] + kept,
        scratch_shapes=[
            pltpu.VMEM((count, width), jnp.bfloat16),
            pltpu.VMEM((count, 2 * inner), jnp.bfloat16),
            pltpu.VMEM((count, 1), jnp.float32),
        ]
        + ([pltpu.SemaphoreType.DMA((2, 3))] if load else []),
        compiler_params=pltpu.CompilerParams(vmem_limit_bytes=VMEM_LIMIT),
        cost_estimate=pl.CostEstimate(
            flops=12 * count * width * inner,
            bytes_accessed=12 * width * inner if load else 4 * count * width,
            transcendentals=2 * count * inner,
        ),
    )(pick, *(pltpu.with_memory_space_constraint(w, pltpu.VMEM) for w in pieces), *held)
    kept = outs[len(sizes) :]
    return outs[: len(sizes)], (kept[:3], kept[3:]) if load else halves


def per_device(
    query, fresh_key_value, kv_cache, cache_lengths, hidden, routes, gates, w_gate_up, w_down
):
    sections = lax.axis_size("sec")
    section = lax.axis_index("sec")
    experts = lax.axis_size("dev") // 2
    expert = lax.axis_index("dev") // 2
    expert_side = section == sections - 1
    count = hidden.shape[0]
    f32 = jnp.float32

    gate_up, down = w_gate_up[0], w_down[0]
    halves = ((gate_up, down), (other_core(gate_up), other_core(down)))

    packed = token_rows(hidden, routes, gates, experts)
    blocks = [to_section(packed, s, sections - 1) for s in range(sections - 1)]
    block = jnp.concatenate(blocks, axis=0)

    held = block.shape[0]
    size = SIDE * held
    cut = 16 * ((size // 2 + 15) // 16)
    lead = cut - 2 * held
    behind, ahead, far = step_u(block, 1), step_u(block, -1), step_u(block, 2)
    group_a, group_b = stacked([block, behind, ahead[:lead]]), stacked([ahead[lead:], far])
    before_a, after_b = step_v(group_a, 1), step_v(group_b, -1)
    before_b, after_a = step_v(group_b, 1), step_v(group_a, -1)
    column = lax.broadcasted_iota(jnp.int32, (1, EXTRA), 1)
    pick = ((column % experts == expert) & (column < 3 * experts)).astype(f32)
    (own_a, own_b), halves = experts_on([group_a, group_b], pick, halves)

    before_a, after_b, before_b, after_a, own_a, own_b = lax.optimization_barrier(
        (before_a, after_b, before_b, after_a, own_a, own_b)
    )
    across_a, across_b = step_v(before_a, 1), step_v(after_b, -1)
    (after_b, before_a), _ = experts_on([after_b, before_a], pick, halves)
    across_a, across_b, after_b, before_a = lax.optimization_barrier((across_a, across_b, after_b, before_a))

    from_after_b, from_before_a = step_v(after_b, 1), step_v(before_a, -1)
    (cross_a, cross_b), _ = experts_on([across_a, across_b], pick, halves)
    from_cross_a, from_cross_b = step_v(cross_a, 1), step_v(cross_b, -1)
    after_a, before_b, from_after_b, from_before_a, cross_a = lax.optimization_barrier(
        (after_a, before_b, from_after_b, from_before_a, cross_a)
    )
    (after_a, before_b), _ = experts_on([after_a, before_b], pick, halves)

    query, _ = lax.optimization_barrier((query, cross_a))
    attention_out = lax.cond(
        expert_side,
        lambda query, *_: jnp.zeros_like(query),
        attention_block,
        query,
        fresh_key_value,
        kv_cache,
        cache_lengths,
    )

    from_before_b = step_v((before_b.astype(f32) + from_cross_b.astype(f32)).astype(jnp.bfloat16), -1)
    from_after_a = step_v((after_a.astype(f32) + from_cross_a.astype(f32)).astype(jnp.bfloat16), 1)
    near = held - lead
    sum_b = own_b.astype(f32) + from_after_b.astype(f32) + from_before_b.astype(f32)
    far = sum_b[near:].astype(jnp.bfloat16)
    part = held // 2
    from_far_a, from_far_b = step_u(far[:part], 1), step_u(far[part:], -1)
    sum_a = own_a.astype(f32) + from_after_a.astype(f32) + from_before_a.astype(f32)
    ahead = jnp.concatenate([sum_a[2 * held :], sum_b[:near]], axis=0)
    ahead = ahead + jnp.pad(from_far_a.astype(f32), ((0, held - part), (0, 0)))
    behind = sum_a[held : 2 * held] + jnp.pad(from_far_b.astype(f32), ((part, 0), (0, 0)))
    total = (
        sum_a[:held]
        + step_u(ahead.astype(jnp.bfloat16), 1).astype(f32)
        + step_u(behind.astype(jnp.bfloat16), -1).astype(f32)
    ).astype(jnp.bfloat16)

    result = None
    for s in range(sections - 1):
        back = to_section(total[s * count : (s + 1) * count], sections - 1, s)
        result = back if result is None else result + back
    return attention_out, result


def solution(mesh):
    return jax.shard_map(
        per_device,
        mesh=mesh,
        in_specs=(
            P(("sec", "dev"), None),
            P(("sec", "dev"), None, None),
            P(("sec", "dev"), None, None, None),
            P(("sec", "dev")),
            P(("sec", "dev"), None),
            P(("sec", "dev"), None),
            P(("sec", "dev"), None),
            P(("sec", "dev"), None, None),
            P(("sec", "dev"), None, None),
        ),
        out_specs=(P(("sec", "dev"), None), P(("sec", "dev"), None)),
        check_vma=False,
    )
```

```python
import functools

import jax
import jax.numpy as jnp
from jax import lax
from jax.experimental import pallas as pl
from jax.experimental.pallas import tpu as pltpu
from jax.sharding import PartitionSpec as P

SIDE = 4
EXTRA = 128
VMEM_LIMIT = 6 << 20


def along(first, distance):
    pairs = []
    for i in range(2 * SIDE * SIDE):
        z, x, core = i // (2 * SIDE), i // 2 % SIDE, i % 2
        if first == (core == 0):
            x = (x + distance) % SIDE
        else:
            z = (z + distance) % SIDE
        pairs.append((i, (z * SIDE + x) * 2 + core))
    return pairs


def step_u(block, distance):
    return lax.ppermute(block, "dev", along(True, distance))


def step_v(block, distance):
    return lax.ppermute(block, "dev", along(False, distance))


def to_section(block, source, target):
    return lax.ppermute(block, "sec", [(source, target)])


def stacked(blocks):
    rows = sum(block.shape[0] for block in blocks)
    start, total = 0, None
    for block in blocks:
        size = block.shape[0]
        padded = jnp.pad(block, ((start, rows - start - size), (0, 0)))
        total = padded if total is None else total + padded
        start += size
    return total


def other_core(block):
    return lax.ppermute(block, "dev", [(i, i ^ 1) for i in range(2 * SIDE * SIDE)])


def attention_block(query, fresh_key_value, kv_cache, cache_lengths):
    count_req = query.shape[0]
    heads_kv = fresh_key_value.shape[1]
    head_size = fresh_key_value.shape[2] // 2
    group_size = query.shape[1] // (heads_kv * head_size)
    query_heads = query.reshape(count_req, heads_kv, group_size, head_size)
    score_scale = head_size ** (-0.5)
    scores = (
        jnp.einsum(
            "rghd,rtgd->rght",
            query_heads,
            kv_cache[..., :head_size],
            preferred_element_type=jnp.float32,
        )
        * score_scale
    )
    valid = jnp.arange(kv_cache.shape[1], dtype=jnp.int32)[None, :] < cache_lengths[:, None]
    scores = jnp.where(valid[:, None, None, :], scores, -jnp.inf)
    own_score = (
        jnp.einsum(
            "rghd,rgd->rgh",
            query_heads,
            fresh_key_value[..., :head_size],
            preferred_element_type=jnp.float32,
        )
        * score_scale
    )
    peak = jnp.maximum(jnp.max(scores, axis=-1), own_score)
    weights = jnp.exp(scores - peak[..., None])
    own_weight = jnp.exp(own_score - peak)
    denominator = jnp.sum(weights, axis=-1) + own_weight
    own_low = lax.optimization_barrier(own_weight.astype(jnp.bfloat16)).astype(jnp.float32)
    mixture = jnp.einsum(
        "rght,rtgd->rghd",
        weights.astype(jnp.bfloat16),
        kv_cache[..., head_size:],
        preferred_element_type=jnp.float32,
    )
    mixture = (
        mixture
        + own_low[..., None] * fresh_key_value[..., head_size:].astype(jnp.float32)[:, :, None, :]
    )
    return (mixture / denominator[..., None]).astype(jnp.bfloat16).reshape(count_req, -1)


def pack_kernel(experts, hidden, routes_in, gates_in, out, routes, gates, sems):
    count, width = hidden.shape
    pairs = ((routes_in, routes), (gates_in, gates), (hidden, out.at[:, :width]))
    copies = [pltpu.make_async_copy(*pair, sems.at[i]) for i, pair in enumerate(pairs)]
    for copy in copies:
        copy.start()
    copies[0].wait()
    copies[1].wait()
    combine = gates[...] / jnp.sum(gates[...], axis=0, keepdims=True)
    place = lax.broadcasted_iota(jnp.int32, (EXTRA, count), 0)
    share = jnp.zeros((EXTRA, count), jnp.float32)
    for k in range(routes.shape[0]):
        named = routes[k : k + 1, :] == place % experts
        share += jnp.where(named, combine[k : k + 1, :], 0.0)
    terms = []
    for _ in range(3):
        terms.append(share.astype(jnp.bfloat16).astype(jnp.float32))
        share = share - terms[-1]
    packed = jnp.where(place < experts, terms[0], jnp.where(place < 2 * experts, terms[1], terms[2]))
    packed = jnp.where(place < 3 * experts, packed, 0.0).astype(jnp.bfloat16)
    same = lax.broadcasted_iota(jnp.int32, (count, count), 0) == lax.broadcasted_iota(
        jnp.int32, (count, count), 1
    )
    turned = lax.dot_general(
        same.astype(jnp.float32).astype(jnp.bfloat16),
        packed,
        (((1,), (1,)), ((), ())),
        preferred_element_type=jnp.float32,
    )
    out[:, width:] = turned.astype(jnp.bfloat16)
    copies[2].wait()


def token_rows(hidden, routes, gates, experts):
    count, width = hidden.shape
    whole = pl.BlockSpec(memory_space=pltpu.VMEM)
    return pl.pallas_call(
        functools.partial(pack_kernel, experts),
        in_specs=[pl.BlockSpec(memory_space=pl.ANY)] * 3,
        out_specs=whole,
        out_shape=jax.ShapeDtypeStruct((count, width + EXTRA), hidden.dtype),
        scratch_shapes=[
            pltpu.VMEM(routes.shape[::-1], routes.dtype),
            pltpu.VMEM(gates.shape[::-1], gates.dtype),
            pltpu.SemaphoreType.DMA((3,)),
        ],
        compiler_params=pltpu.CompilerParams(vmem_limit_bytes=VMEM_LIMIT),
    )(*(pltpu.with_memory_space_constraint(w, pltpu.HBM) for w in (hidden, routes.T, gates.T)))


def weight_copies(gate_up, down, kept, sems):
    inner = down.shape[0]
    sources = (gate_up.at[:, :inner], gate_up.at[:, inner:], down)
    return [pltpu.make_async_copy(*pair, sems.at[i]) for i, pair in enumerate(zip(sources, kept))]


def kept_shapes(gate_up, down):
    inner, width = down.shape
    shapes = [(width, inner), (width, inner), (inner, width)]
    return [pltpu.VMEM(shape, down.dtype) for shape in shapes]


def expert_kernel(pieces, columns, load, *refs):
    refs = list(refs)
    pick = refs.pop(0)
    rows_in = [refs.pop(0) for _ in range(pieces)]
    halves = [[refs.pop(0) for _ in range(2 if load else 3)] for _ in range(2)]
    outs = [refs.pop(0) for _ in range(pieces)]
    copies = []
    if load:
        kept = [[refs.pop(0) for _ in range(3)] for _ in range(2)]
        sems = refs.pop()
        for half in range(2):
            copies += weight_copies(*halves[half], kept[half], sems.at[half])
        halves = kept
        for index in (0, 1, 3, 4, 2, 5):
            copies[index].start()
    rows, act, share = refs
    inner, width = halves[0][2].shape

    def arrived(index):
        if load:
            copies[index].wait()

    start = 0
    for ref in rows_in:
        size = ref.shape[0]
        rows[start : start + size, :] = ref[:, :width]
        share[start : start + size, :] = jnp.sum(
            ref[:, width:].astype(jnp.float32) * pick[...], axis=1, keepdims=True
        )
        start += size

    for half, (gate, up, _) in enumerate(halves):
        arrived(3 * half)
        left = jnp.dot(rows[...], gate[...], preferred_element_type=jnp.float32)
        arrived(3 * half + 1)
        right = jnp.dot(rows[...], up[...], preferred_element_type=jnp.float32)
        act[:, half * inner : (half + 1) * inner] = (jax.nn.silu(left) * right).astype(jnp.bfloat16)
    arrived(2)
    arrived(5)

    @pl.loop(0, width // columns)
    def _(n):
        at = pl.ds(pl.multiple_of(n * columns, columns), columns)
        total = jnp.dot(act[:, :inner], halves[0][2][:, at], preferred_element_type=jnp.float32)
        total += jnp.dot(act[:, inner:], halves[1][2][:, at], preferred_element_type=jnp.float32)
        total = (total * share[...]).astype(jnp.bfloat16)
        start = 0
        for out in outs:
            out[:, at] = total[start : start + out.shape[0], :]
            start += out.shape[0]


def experts_on(pieces, pick, halves):
    inner, width = halves[0][-1].shape
    load = len(halves[0]) == 2
    sizes = [piece.shape[0] for piece in pieces]
    count = sum(sizes)
    whole = pl.BlockSpec(memory_space=pltpu.VMEM)
    space = pl.BlockSpec(memory_space=pl.ANY) if load else whole
    constraint = pltpu.HBM if load else pltpu.VMEM
    held = [pltpu.with_memory_space_constraint(w, constraint) for half in halves for w in half]
    kept = [shape for half in halves for shape in kept_shapes(*half)] if load else []
    outs = pl.pallas_call(
        functools.partial(expert_kernel, len(pieces), 1024, load),
        in_specs=[whole] * (1 + len(pieces)) + [space] * len(held),
        out_specs=[whole] * (len(sizes) + len(kept)),
        out_shape=[jax.ShapeDtypeStruct((size, width), jnp.bfloat16) for size in sizes] + kept,
        scratch_shapes=[
            pltpu.VMEM((count, width), jnp.bfloat16),
            pltpu.VMEM((count, 2 * inner), jnp.bfloat16),
            pltpu.VMEM((count, 1), jnp.float32),
        ]
        + ([pltpu.SemaphoreType.DMA((2, 3))] if load else []),
        compiler_params=pltpu.CompilerParams(vmem_limit_bytes=VMEM_LIMIT),
        cost_estimate=pl.CostEstimate(
            flops=12 * count * width * inner,
            bytes_accessed=12 * width * inner if load else 4 * count * width,
            transcendentals=2 * count * inner,
        ),
    )(pick, *(pltpu.with_memory_space_constraint(w, pltpu.VMEM) for w in pieces), *held)
    kept = outs[len(sizes) :]
    return outs[: len(sizes)], (kept[:3], kept[3:]) if load else halves


def per_device(
    query, fresh_key_value, kv_cache, cache_lengths, hidden, routes, gates, w_gate_up, w_down
):
    sections = lax.axis_size("sec")
    section = lax.axis_index("sec")
    experts = lax.axis_size("dev") // 2
    expert = lax.axis_index("dev") // 2
    expert_side = section == sections - 1
    count = hidden.shape[0]
    f32 = jnp.float32

    gate_up, down = w_gate_up[0], w_down[0]
    halves = ((gate_up, down), (other_core(gate_up), other_core(down)))

    packed = token_rows(hidden, routes, gates, experts)
    blocks = [to_section(packed, s, sections - 1) for s in range(sections - 1)]
    block = jnp.concatenate(blocks, axis=0)

    held = block.shape[0]
    size = SIDE * held
    cut = 16 * ((size // 2 + 15) // 16)
    lead = cut - 2 * held
    part = held // 2
    behind, ahead = step_u(block, 1), step_u(block, -1)
    far_a, far_b = step_u(behind[:part], 1), step_u(ahead[part:], -1)
    group_a, group_b = stacked([block, behind, ahead[:lead]]), stacked([ahead[lead:], far_a, far_b])
    before_a, after_b = step_v(group_a, 1), step_v(group_b, -1)
    before_b, after_a = step_v(group_b, 1), step_v(group_a, -1)
    column = lax.broadcasted_iota(jnp.int32, (1, EXTRA), 1)
    pick = ((column % experts == expert) & (column < 3 * experts)).astype(f32)
    (own_a, own_b), halves = experts_on([group_a, group_b], pick, halves)

    before_a, after_b, before_b, after_a, own_a, own_b = lax.optimization_barrier(
        (before_a, after_b, before_b, after_a, own_a, own_b)
    )
    across_a, across_b = step_v(before_a, 1), step_v(after_b, -1)
    (after_b, before_a), _ = experts_on([after_b, before_a], pick, halves)
    across_a, across_b, after_b, before_a = lax.optimization_barrier((across_a, across_b, after_b, before_a))

    from_after_b, from_before_a = step_v(after_b, 1), step_v(before_a, -1)
    (cross_a, cross_b), _ = experts_on([across_a, across_b], pick, halves)
    from_cross_a, from_cross_b = step_v(cross_a, 1), step_v(cross_b, -1)
    after_a, before_b, from_after_b, from_before_a, cross_a = lax.optimization_barrier(
        (after_a, before_b, from_after_b, from_before_a, cross_a)
    )
    (after_a, before_b), _ = experts_on([after_a, before_b], pick, halves)

    query, _ = lax.optimization_barrier((query, cross_a))
    attention_out = lax.cond(
        expert_side,
        lambda query, *_: jnp.zeros_like(query),
        attention_block,
        query,
        fresh_key_value,
        kv_cache,
        cache_lengths,
    )

    from_before_b = step_v((before_b.astype(f32) + from_cross_b.astype(f32)).astype(jnp.bfloat16), -1)
    from_after_a = step_v((after_a.astype(f32) + from_cross_a.astype(f32)).astype(jnp.bfloat16), 1)
    near = held - lead
    sum_b = own_b.astype(f32) + from_after_b.astype(f32) + from_before_b.astype(f32)
    far = sum_b[near:].astype(jnp.bfloat16)
    from_far_a, from_far_b = step_u(far[:part], 1), step_u(far[part:], -1)
    sum_a = own_a.astype(f32) + from_after_a.astype(f32) + from_before_a.astype(f32)
    ahead = jnp.concatenate([sum_a[2 * held :], sum_b[:near]], axis=0)
    ahead = ahead + jnp.pad(from_far_a.astype(f32), ((0, held - part), (0, 0)))
    behind = sum_a[held : 2 * held] + jnp.pad(from_far_b.astype(f32), ((part, 0), (0, 0)))
    total = (
        sum_a[:held]
        + step_u(ahead.astype(jnp.bfloat16), 1).astype(f32)
        + step_u(behind.astype(jnp.bfloat16), -1).astype(f32)
    ).astype(jnp.bfloat16)

    result = None
    for s in range(sections - 1):
        back = to_section(total[s * count : (s + 1) * count], sections - 1, s)
        result = back if result is None else result + back
    return attention_out, result


def solution(mesh):
    return jax.shard_map(
        per_device,
        mesh=mesh,
        in_specs=(
            P(("sec", "dev"), None),
            P(("sec", "dev"), None, None),
            P(("sec", "dev"), None, None, None),
            P(("sec", "dev")),
            P(("sec", "dev"), None),
            P(("sec", "dev"), None),
            P(("sec", "dev"), None),
            P(("sec", "dev"), None, None),
            P(("sec", "dev"), None, None),
        ),
        out_specs=(P(("sec", "dev"), None), P(("sec", "dev"), None)),
        check_vma=False,
    )
```

```python
import functools

import jax
import jax.numpy as jnp
from jax import lax
from jax.experimental import pallas as pl
from jax.experimental.pallas import tpu as pltpu
from jax.sharding import PartitionSpec as P

SIDE = 4
EXTRA = 128
VMEM_LIMIT = 6 << 20


def along(first, distance):
    pairs = []
    for i in range(2 * SIDE * SIDE):
        z, x, core = i // (2 * SIDE), i // 2 % SIDE, i % 2
        if first == (core == 0):
            x = (x + distance) % SIDE
        else:
            z = (z + distance) % SIDE
        pairs.append((i, (z * SIDE + x) * 2 + core))
    return pairs


def step_u(block, distance):
    return lax.ppermute(block, "dev", along(True, distance))


def step_v(block, distance):
    return lax.ppermute(block, "dev", along(False, distance))


def to_section(block, source, target):
    return lax.ppermute(block, "sec", [(source, target)])


def stacked(blocks):
    rows = sum(block.shape[0] for block in blocks)
    start, total = 0, None
    for block in blocks:
        size = block.shape[0]
        padded = jnp.pad(block, ((start, rows - start - size), (0, 0)))
        total = padded if total is None else total + padded
        start += size
    return total


def other_core(block):
    return lax.ppermute(block, "dev", [(i, i ^ 1) for i in range(2 * SIDE * SIDE)])


def attention_block(query, fresh_key_value, kv_cache, cache_lengths):
    count_req = query.shape[0]
    heads_kv = fresh_key_value.shape[1]
    head_size = fresh_key_value.shape[2] // 2
    group_size = query.shape[1] // (heads_kv * head_size)
    query_heads = query.reshape(count_req, heads_kv, group_size, head_size)
    score_scale = head_size ** (-0.5)
    scores = (
        jnp.einsum(
            "rghd,rtgd->rght",
            query_heads,
            kv_cache[..., :head_size],
            preferred_element_type=jnp.float32,
        )
        * score_scale
    )
    valid = jnp.arange(kv_cache.shape[1], dtype=jnp.int32)[None, :] < cache_lengths[:, None]
    scores = jnp.where(valid[:, None, None, :], scores, -jnp.inf)
    own_score = (
        jnp.einsum(
            "rghd,rgd->rgh",
            query_heads,
            fresh_key_value[..., :head_size],
            preferred_element_type=jnp.float32,
        )
        * score_scale
    )
    peak = jnp.maximum(jnp.max(scores, axis=-1), own_score)
    weights = jnp.exp(scores - peak[..., None])
    own_weight = jnp.exp(own_score - peak)
    denominator = jnp.sum(weights, axis=-1) + own_weight
    own_low = lax.optimization_barrier(own_weight.astype(jnp.bfloat16)).astype(jnp.float32)
    mixture = jnp.einsum(
        "rght,rtgd->rghd",
        weights.astype(jnp.bfloat16),
        kv_cache[..., head_size:],
        preferred_element_type=jnp.float32,
    )
    mixture = (
        mixture
        + own_low[..., None] * fresh_key_value[..., head_size:].astype(jnp.float32)[:, :, None, :]
    )
    return (mixture / denominator[..., None]).astype(jnp.bfloat16).reshape(count_req, -1)


def pack_kernel(experts, hidden, routes_in, gates_in, out, routes, gates, sems):
    count, width = hidden.shape
    pairs = ((routes_in, routes), (gates_in, gates), (hidden, out.at[:, :width]))
    copies = [pltpu.make_async_copy(*pair, sems.at[i]) for i, pair in enumerate(pairs)]
    for copy in copies:
        copy.start()
    copies[0].wait()
    copies[1].wait()
    combine = gates[...] / jnp.sum(gates[...], axis=0, keepdims=True)
    place = lax.broadcasted_iota(jnp.int32, (EXTRA, count), 0)
    share = jnp.zeros((EXTRA, count), jnp.float32)
    for k in range(routes.shape[0]):
        named = routes[k : k + 1, :] == place % experts
        share += jnp.where(named, combine[k : k + 1, :], 0.0)
    terms = []
    for _ in range(3):
        terms.append(share.astype(jnp.bfloat16).astype(jnp.float32))
        share = share - terms[-1]
    packed = jnp.where(place < experts, terms[0], jnp.where(place < 2 * experts, terms[1], terms[2]))
    packed = jnp.where(place < 3 * experts, packed, 0.0).astype(jnp.bfloat16)
    same = lax.broadcasted_iota(jnp.int32, (count, count), 0) == lax.broadcasted_iota(
        jnp.int32, (count, count), 1
    )
    turned = lax.dot_general(
        same.astype(jnp.float32).astype(jnp.bfloat16),
        packed,
        (((1,), (1,)), ((), ())),
        preferred_element_type=jnp.float32,
    )
    out[:, width:] = turned.astype(jnp.bfloat16)
    copies[2].wait()


def token_rows(hidden, routes, gates, experts):
    count, width = hidden.shape
    whole = pl.BlockSpec(memory_space=pltpu.VMEM)
    return pl.pallas_call(
        functools.partial(pack_kernel, experts),
        in_specs=[pl.BlockSpec(memory_space=pl.ANY)] * 3,
        out_specs=whole,
        out_shape=jax.ShapeDtypeStruct((count, width + EXTRA), hidden.dtype),
        scratch_shapes=[
            pltpu.VMEM(routes.shape[::-1], routes.dtype),
            pltpu.VMEM(gates.shape[::-1], gates.dtype),
            pltpu.SemaphoreType.DMA((3,)),
        ],
        compiler_params=pltpu.CompilerParams(vmem_limit_bytes=VMEM_LIMIT),
    )(*(pltpu.with_memory_space_constraint(w, pltpu.HBM) for w in (hidden, routes.T, gates.T)))


def weight_copies(gate_up, down, kept, sems):
    inner = down.shape[0]
    sources = (gate_up.at[:, :inner], gate_up.at[:, inner:], down)
    return [pltpu.make_async_copy(*pair, sems.at[i]) for i, pair in enumerate(zip(sources, kept))]


def kept_shapes(gate_up, down):
    inner, width = down.shape
    shapes = [(width, inner), (width, inner), (inner, width)]
    return [pltpu.VMEM(shape, down.dtype) for shape in shapes]


def expert_kernel(pieces, columns, load, *refs):
    refs = list(refs)
    pick = refs.pop(0)
    rows_in = [refs.pop(0) for _ in range(pieces)]
    halves = [[refs.pop(0) for _ in range(2 if load else 3)] for _ in range(2)]
    outs = [refs.pop(0) for _ in range(pieces)]
    copies = []
    if load:
        kept = [[refs.pop(0) for _ in range(3)] for _ in range(2)]
        sems = refs.pop()
        for half in range(2):
            copies += weight_copies(*halves[half], kept[half], sems.at[half])
        halves = kept
        for index in (0, 1, 3, 4, 2, 5):
            copies[index].start()
    rows, act, share = refs
    inner, width = halves[0][2].shape

    def arrived(index):
        if load:
            copies[index].wait()

    start = 0
    for ref in rows_in:
        size = ref.shape[0]
        rows[start : start + size, :] = ref[:, :width]
        share[start : start + size, :] = jnp.sum(
            ref[:, width:].astype(jnp.float32) * pick[...], axis=1, keepdims=True
        )
        start += size

    for half, (gate, up, _) in enumerate(halves):
        arrived(3 * half)
        left = jnp.dot(rows[...], gate[...], preferred_element_type=jnp.float32)
        arrived(3 * half + 1)
        right = jnp.dot(rows[...], up[...], preferred_element_type=jnp.float32)
        act[:, half * inner : (half + 1) * inner] = (jax.nn.silu(left) * right).astype(jnp.bfloat16)
    arrived(2)
    arrived(5)

    @pl.loop(0, width // columns)
    def _(n):
        at = pl.ds(pl.multiple_of(n * columns, columns), columns)
        total = jnp.dot(act[:, :inner], halves[0][2][:, at], preferred_element_type=jnp.float32)
        total += jnp.dot(act[:, inner:], halves[1][2][:, at], preferred_element_type=jnp.float32)
        total = (total * share[...]).astype(jnp.bfloat16)
        start = 0
        for out in outs:
            out[:, at] = total[start : start + out.shape[0], :]
            start += out.shape[0]


def experts_on(pieces, pick, halves):
    inner, width = halves[0][-1].shape
    load = len(halves[0]) == 2
    sizes = [piece.shape[0] for piece in pieces]
    count = sum(sizes)
    whole = pl.BlockSpec(memory_space=pltpu.VMEM)
    space = pl.BlockSpec(memory_space=pl.ANY) if load else whole
    constraint = pltpu.HBM if load else pltpu.VMEM
    held = [pltpu.with_memory_space_constraint(w, constraint) for half in halves for w in half]
    kept = [shape for half in halves for shape in kept_shapes(*half)] if load else []
    outs = pl.pallas_call(
        functools.partial(expert_kernel, len(pieces), 1024, load),
        in_specs=[whole] * (1 + len(pieces)) + [space] * len(held),
        out_specs=[whole] * (len(sizes) + len(kept)),
        out_shape=[jax.ShapeDtypeStruct((size, width), jnp.bfloat16) for size in sizes] + kept,
        scratch_shapes=[
            pltpu.VMEM((count, width), jnp.bfloat16),
            pltpu.VMEM((count, 2 * inner), jnp.bfloat16),
            pltpu.VMEM((count, 1), jnp.float32),
        ]
        + ([pltpu.SemaphoreType.DMA((2, 3))] if load else []),
        compiler_params=pltpu.CompilerParams(vmem_limit_bytes=VMEM_LIMIT),
        cost_estimate=pl.CostEstimate(
            flops=12 * count * width * inner,
            bytes_accessed=12 * width * inner if load else 4 * count * width,
            transcendentals=2 * count * inner,
        ),
    )(pick, *(pltpu.with_memory_space_constraint(w, pltpu.VMEM) for w in pieces), *held)
    kept = outs[len(sizes) :]
    return outs[: len(sizes)], (kept[:3], kept[3:]) if load else halves


def per_device(
    query, fresh_key_value, kv_cache, cache_lengths, hidden, routes, gates, w_gate_up, w_down
):
    sections = lax.axis_size("sec")
    section = lax.axis_index("sec")
    experts = lax.axis_size("dev") // 2
    expert = lax.axis_index("dev") // 2
    expert_side = section == sections - 1
    count = hidden.shape[0]
    f32 = jnp.float32

    gate_up, down = w_gate_up[0], w_down[0]
    halves = ((gate_up, down), (other_core(gate_up), other_core(down)))

    packed = token_rows(hidden, routes, gates, experts)
    blocks = [to_section(packed, s, sections - 1) for s in range(sections - 1)]
    block = jnp.concatenate(blocks, axis=0)

    held = block.shape[0]
    size = SIDE * held
    cut = 16 * ((size // 2 + 15) // 16)
    lead = cut - 2 * held
    behind, ahead, far = step_u(block, 1), step_u(block, -1), step_u(block, 2)
    group_a, group_b = stacked([block, behind, ahead[:lead]]), stacked([ahead[lead:], far])
    before_a, after_b = step_v(group_a, 1), step_v(group_b, -1)
    column = lax.broadcasted_iota(jnp.int32, (1, EXTRA), 1)
    pick = ((column % experts == expert) & (column < 3 * experts)).astype(f32)
    (own_a, own_b), halves = experts_on([group_a, group_b], pick, halves)

    before_a, after_b, group_a, group_b, own_a, own_b = lax.optimization_barrier(
        (before_a, after_b, group_a, group_b, own_a, own_b)
    )
    across_a, across_b = step_v(before_a, 1), step_v(after_b, -1)
    before_b, after_a = step_v(group_b, 1), step_v(group_a, -1)
    (after_b, before_a), _ = experts_on([after_b, before_a], pick, halves)
    across_a, across_b, after_b, before_a = lax.optimization_barrier((across_a, across_b, after_b, before_a))

    from_after_b, from_before_a = step_v(after_b, 1), step_v(before_a, -1)
    (cross_a, cross_b), _ = experts_on([across_a, across_b], pick, halves)
    from_cross_a, from_cross_b = step_v(cross_a, 1), step_v(cross_b, -1)
    after_a, before_b, from_after_b, from_before_a, cross_a = lax.optimization_barrier(
        (after_a, before_b, from_after_b, from_before_a, cross_a)
    )
    (after_a, before_b), _ = experts_on([after_a, before_b], pick, halves)

    query, _ = lax.optimization_barrier((query, cross_a))
    attention_out = lax.cond(
        expert_side,
        lambda query, *_: jnp.zeros_like(query),
        attention_block,
        query,
        fresh_key_value,
        kv_cache,
        cache_lengths,
    )

    from_before_b = step_v((before_b.astype(f32) + from_cross_b.astype(f32)).astype(jnp.bfloat16), -1)
    from_after_a = step_v((after_a.astype(f32) + from_cross_a.astype(f32)).astype(jnp.bfloat16), 1)
    near = held - lead
    sum_b = own_b.astype(f32) + from_after_b.astype(f32) + from_before_b.astype(f32)
    far = sum_b[near:].astype(jnp.bfloat16)
    part = held // 2
    from_far_a, from_far_b = step_u(far[:part], 1), step_u(far[part:], -1)
    sum_a = own_a.astype(f32) + from_after_a.astype(f32) + from_before_a.astype(f32)
    ahead = jnp.concatenate([sum_a[2 * held :], sum_b[:near]], axis=0)
    ahead = ahead + jnp.pad(from_far_a.astype(f32), ((0, held - part), (0, 0)))
    behind = sum_a[held : 2 * held] + jnp.pad(from_far_b.astype(f32), ((part, 0), (0, 0)))
    total = (
        sum_a[:held]
        + step_u(ahead.astype(jnp.bfloat16), 1).astype(f32)
        + step_u(behind.astype(jnp.bfloat16), -1).astype(f32)
    ).astype(jnp.bfloat16)

    result = None
    for s in range(sections - 1):
        back = to_section(total[s * count : (s + 1) * count], sections - 1, s)
        result = back if result is None else result + back
    return attention_out, result


def solution(mesh):
    return jax.shard_map(
        per_device,
        mesh=mesh,
        in_specs=(
            P(("sec", "dev"), None),
            P(("sec", "dev"), None, None),
            P(("sec", "dev"), None, None, None),
            P(("sec", "dev")),
            P(("sec", "dev"), None),
            P(("sec", "dev"), None),
            P(("sec", "dev"), None),
            P(("sec", "dev"), None, None),
            P(("sec", "dev"), None, None),
        ),
        out_specs=(P(("sec", "dev"), None), P(("sec", "dev"), None)),
        check_vma=False,
    )
```

```python
import functools

import jax
import jax.numpy as jnp
from jax import lax
from jax.experimental import pallas as pl
from jax.experimental.pallas import tpu as pltpu
from jax.sharding import PartitionSpec as P

SIDE = 4
EXTRA = 128
VMEM_LIMIT = 6 << 20


def along(first, distance):
    pairs = []
    for i in range(2 * SIDE * SIDE):
        z, x, core = i // (2 * SIDE), i // 2 % SIDE, i % 2
        if first == (core == 0):
            x = (x + distance) % SIDE
        else:
            z = (z + distance) % SIDE
        pairs.append((i, (z * SIDE + x) * 2 + core))
    return pairs


def step_u(block, distance):
    return lax.ppermute(block, "dev", along(True, distance))


def step_v(block, distance):
    return lax.ppermute(block, "dev", along(False, distance))


def to_section(block, source, target):
    return lax.ppermute(block, "sec", [(source, target)])


def stacked(blocks):
    rows = sum(block.shape[0] for block in blocks)
    start, total = 0, None
    for block in blocks:
        size = block.shape[0]
        padded = jnp.pad(block, ((start, rows - start - size), (0, 0)))
        total = padded if total is None else total + padded
        start += size
    return total


def other_core(block):
    return lax.ppermute(block, "dev", [(i, i ^ 1) for i in range(2 * SIDE * SIDE)])


def attention_block(query, fresh_key_value, kv_cache, cache_lengths):
    count_req = query.shape[0]
    heads_kv = fresh_key_value.shape[1]
    head_size = fresh_key_value.shape[2] // 2
    group_size = query.shape[1] // (heads_kv * head_size)
    query_heads = query.reshape(count_req, heads_kv, group_size, head_size)
    score_scale = head_size ** (-0.5)
    scores = (
        jnp.einsum(
            "rghd,rtgd->rght",
            query_heads,
            kv_cache[..., :head_size],
            preferred_element_type=jnp.float32,
        )
        * score_scale
    )
    valid = jnp.arange(kv_cache.shape[1], dtype=jnp.int32)[None, :] < cache_lengths[:, None]
    scores = jnp.where(valid[:, None, None, :], scores, -jnp.inf)
    own_score = (
        jnp.einsum(
            "rghd,rgd->rgh",
            query_heads,
            fresh_key_value[..., :head_size],
            preferred_element_type=jnp.float32,
        )
        * score_scale
    )
    peak = jnp.maximum(jnp.max(scores, axis=-1), own_score)
    weights = jnp.exp(scores - peak[..., None])
    own_weight = jnp.exp(own_score - peak)
    denominator = jnp.sum(weights, axis=-1) + own_weight
    own_low = lax.optimization_barrier(own_weight.astype(jnp.bfloat16)).astype(jnp.float32)
    mixture = jnp.einsum(
        "rght,rtgd->rghd",
        weights.astype(jnp.bfloat16),
        kv_cache[..., head_size:],
        preferred_element_type=jnp.float32,
    )
    mixture = (
        mixture
        + own_low[..., None] * fresh_key_value[..., head_size:].astype(jnp.float32)[:, :, None, :]
    )
    return (mixture / denominator[..., None]).astype(jnp.bfloat16).reshape(count_req, -1)


def pack_kernel(experts, hidden, routes_in, gates_in, out, routes, gates, sems):
    count, width = hidden.shape
    pairs = ((routes_in, routes), (gates_in, gates), (hidden, out.at[:, :width]))
    copies = [pltpu.make_async_copy(*pair, sems.at[i]) for i, pair in enumerate(pairs)]
    for copy in copies:
        copy.start()
    copies[0].wait()
    copies[1].wait()
    combine = gates[...] / jnp.sum(gates[...], axis=0, keepdims=True)
    place = lax.broadcasted_iota(jnp.int32, (EXTRA, count), 0)
    share = jnp.zeros((EXTRA, count), jnp.float32)
    for k in range(routes.shape[0]):
        named = routes[k : k + 1, :] == place % experts
        share += jnp.where(named, combine[k : k + 1, :], 0.0)
    terms = []
    for _ in range(3):
        terms.append(share.astype(jnp.bfloat16).astype(jnp.float32))
        share = share - terms[-1]
    packed = jnp.where(place < experts, terms[0], jnp.where(place < 2 * experts, terms[1], terms[2]))
    packed = jnp.where(place < 3 * experts, packed, 0.0).astype(jnp.bfloat16)
    same = lax.broadcasted_iota(jnp.int32, (count, count), 0) == lax.broadcasted_iota(
        jnp.int32, (count, count), 1
    )
    turned = lax.dot_general(
        same.astype(jnp.float32).astype(jnp.bfloat16),
        packed,
        (((1,), (1,)), ((), ())),
        preferred_element_type=jnp.float32,
    )
    out[:, width:] = turned.astype(jnp.bfloat16)
    copies[2].wait()


def token_rows(hidden, routes, gates, experts):
    count, width = hidden.shape
    whole = pl.BlockSpec(memory_space=pltpu.VMEM)
    return pl.pallas_call(
        functools.partial(pack_kernel, experts),
        in_specs=[pl.BlockSpec(memory_space=pl.ANY)] * 3,
        out_specs=whole,
        out_shape=jax.ShapeDtypeStruct((count, width + EXTRA), hidden.dtype),
        scratch_shapes=[
            pltpu.VMEM(routes.shape[::-1], routes.dtype),
            pltpu.VMEM(gates.shape[::-1], gates.dtype),
            pltpu.SemaphoreType.DMA((3,)),
        ],
        compiler_params=pltpu.CompilerParams(vmem_limit_bytes=VMEM_LIMIT),
    )(*(pltpu.with_memory_space_constraint(w, pltpu.HBM) for w in (hidden, routes.T, gates.T)))


def weight_copies(gate_up, down, kept, sems):
    inner = down.shape[0]
    sources = (gate_up.at[:, :inner], gate_up.at[:, inner:], down)
    return [pltpu.make_async_copy(*pair, sems.at[i]) for i, pair in enumerate(zip(sources, kept))]


def kept_shapes(gate_up, down):
    inner, width = down.shape
    shapes = [(width, inner), (width, inner), (inner, width)]
    return [pltpu.VMEM(shape, down.dtype) for shape in shapes]


def expert_kernel(pieces, columns, load, serving, *refs):
    @pl.when(serving[0] > 0)
    def _():
        expert_rows(pieces, columns, load, *refs)


def expert_rows(pieces, columns, load, *refs):
    refs = list(refs)
    pick = refs.pop(0)
    rows_in = [refs.pop(0) for _ in range(pieces)]
    halves = [[refs.pop(0) for _ in range(2 if load else 3)] for _ in range(2)]
    outs = [refs.pop(0) for _ in range(pieces)]
    copies = []
    if load:
        kept = [[refs.pop(0) for _ in range(3)] for _ in range(2)]
        sems = refs.pop()
        for half in range(2):
            copies += weight_copies(*halves[half], kept[half], sems.at[half])
        halves = kept
        for index in (0, 1, 3, 4, 2, 5):
            copies[index].start()
    rows, act, share = refs
    inner, width = halves[0][2].shape

    def arrived(index):
        if load:
            copies[index].wait()

    start = 0
    for ref in rows_in:
        size = ref.shape[0]
        rows[start : start + size, :] = ref[:, :width]
        share[start : start + size, :] = jnp.sum(
            ref[:, width:].astype(jnp.float32) * pick[...], axis=1, keepdims=True
        )
        start += size

    for half, (gate, up, _) in enumerate(halves):
        arrived(3 * half)
        left = jnp.dot(rows[...], gate[...], preferred_element_type=jnp.float32)
        arrived(3 * half + 1)
        right = jnp.dot(rows[...], up[...], preferred_element_type=jnp.float32)
        act[:, half * inner : (half + 1) * inner] = (jax.nn.silu(left) * right).astype(jnp.bfloat16)
    arrived(2)
    arrived(5)

    @pl.loop(0, width // columns)
    def _(n):
        at = pl.ds(pl.multiple_of(n * columns, columns), columns)
        total = jnp.dot(act[:, :inner], halves[0][2][:, at], preferred_element_type=jnp.float32)
        total += jnp.dot(act[:, inner:], halves[1][2][:, at], preferred_element_type=jnp.float32)
        total = (total * share[...]).astype(jnp.bfloat16)
        start = 0
        for out in outs:
            out[:, at] = total[start : start + out.shape[0], :]
            start += out.shape[0]


def experts_on(pieces, serving, pick, halves):
    inner, width = halves[0][-1].shape
    load = len(halves[0]) == 2
    sizes = [piece.shape[0] for piece in pieces]
    count = sum(sizes)
    whole = pl.BlockSpec(memory_space=pltpu.VMEM)
    space = pl.BlockSpec(memory_space=pl.ANY) if load else whole
    constraint = pltpu.HBM if load else pltpu.VMEM
    held = [pltpu.with_memory_space_constraint(w, constraint) for half in halves for w in half]
    kept = [shape for half in halves for shape in kept_shapes(*half)] if load else []
    outs = pl.pallas_call(
        functools.partial(expert_kernel, len(pieces), 1024, load),
        in_specs=[pl.BlockSpec(memory_space=pltpu.SMEM)] + [whole] * (1 + len(pieces)) + [space] * len(held),
        out_specs=[whole] * (len(sizes) + len(kept)),
        out_shape=[jax.ShapeDtypeStruct((size, width), jnp.bfloat16) for size in sizes] + kept,
        scratch_shapes=[
            pltpu.VMEM((count, width), jnp.bfloat16),
            pltpu.VMEM((count, 2 * inner), jnp.bfloat16),
            pltpu.VMEM((count, 1), jnp.float32),
        ]
        + ([pltpu.SemaphoreType.DMA((2, 3))] if load else []),
        compiler_params=pltpu.CompilerParams(vmem_limit_bytes=VMEM_LIMIT),
        cost_estimate=pl.CostEstimate(
            flops=12 * count * width * inner,
            bytes_accessed=12 * width * inner if load else 4 * count * width,
            transcendentals=2 * count * inner,
        ),
    )(serving, pick, *(pltpu.with_memory_space_constraint(w, pltpu.VMEM) for w in pieces), *held)
    kept = outs[len(sizes) :]
    return outs[: len(sizes)], (kept[:3], kept[3:]) if load else halves


def per_device(
    query, fresh_key_value, kv_cache, cache_lengths, hidden, routes, gates, w_gate_up, w_down
):
    sections = lax.axis_size("sec")
    section = lax.axis_index("sec")
    experts = lax.axis_size("dev") // 2
    expert = lax.axis_index("dev") // 2
    expert_side = section == sections - 1
    count = hidden.shape[0]
    f32 = jnp.float32

    gate_up, down = w_gate_up[0], w_down[0]
    halves = ((gate_up, down), (other_core(gate_up), other_core(down)))

    packed = token_rows(hidden, routes, gates, experts)
    blocks = [to_section(packed, s, sections - 1) for s in range(sections - 1)]
    block = jnp.concatenate(blocks, axis=0)

    held = block.shape[0]
    size = SIDE * held
    cut = 16 * ((size // 2 + 15) // 16)
    lead = cut - 2 * held
    behind, ahead, far = step_u(block, 1), step_u(block, -1), step_u(block, 2)
    group_a, group_b = stacked([block, behind, ahead[:lead]]), stacked([ahead[lead:], far])
    before_a, after_b = step_v(group_a, 1), step_v(group_b, -1)
    before_b, after_a = step_v(group_b, 1), step_v(group_a, -1)
    column = lax.broadcasted_iota(jnp.int32, (1, EXTRA), 1)
    pick = ((column % experts == expert) & (column < 3 * experts)).astype(f32)
    serving = expert_side.astype(jnp.int32).reshape(1)
    (own_a, own_b), halves = experts_on([group_a, group_b], serving, pick, halves)

    before_a, after_b, before_b, after_a, own_a, own_b = lax.optimization_barrier(
        (before_a, after_b, before_b, after_a, own_a, own_b)
    )
    across_a, across_b = step_v(before_a, 1), step_v(after_b, -1)
    (after_b, before_a), _ = experts_on([after_b, before_a], serving, pick, halves)
    across_a, across_b, after_b, before_a = lax.optimization_barrier((across_a, across_b, after_b, before_a))

    from_after_b, from_before_a = step_v(after_b, 1), step_v(before_a, -1)
    (cross_a, cross_b), _ = experts_on([across_a, across_b], serving, pick, halves)
    from_cross_a, from_cross_b = step_v(cross_a, 1), step_v(cross_b, -1)
    after_a, before_b, from_after_b, from_before_a, cross_a = lax.optimization_barrier(
        (after_a, before_b, from_after_b, from_before_a, cross_a)
    )
    (after_a, before_b), _ = experts_on([after_a, before_b], serving, pick, halves)

    query, _ = lax.optimization_barrier((query, cross_a))
    attention_out = lax.cond(
        expert_side,
        lambda query, *_: jnp.zeros_like(query),
        attention_block,
        query,
        fresh_key_value,
        kv_cache,
        cache_lengths,
    )

    from_before_b = step_v((before_b.astype(f32) + from_cross_b.astype(f32)).astype(jnp.bfloat16), -1)
    from_after_a = step_v((after_a.astype(f32) + from_cross_a.astype(f32)).astype(jnp.bfloat16), 1)
    near = held - lead
    sum_b = own_b.astype(f32) + from_after_b.astype(f32) + from_before_b.astype(f32)
    far = sum_b[near:].astype(jnp.bfloat16)
    part = held // 2
    from_far_a, from_far_b = step_u(far[:part], 1), step_u(far[part:], -1)
    sum_a = own_a.astype(f32) + from_after_a.astype(f32) + from_before_a.astype(f32)
    ahead = jnp.concatenate([sum_a[2 * held :], sum_b[:near]], axis=0)
    ahead = ahead + jnp.pad(from_far_a.astype(f32), ((0, held - part), (0, 0)))
    behind = sum_a[held : 2 * held] + jnp.pad(from_far_b.astype(f32), ((part, 0), (0, 0)))
    total = (
        sum_a[:held]
        + step_u(ahead.astype(jnp.bfloat16), 1).astype(f32)
        + step_u(behind.astype(jnp.bfloat16), -1).astype(f32)
    ).astype(jnp.bfloat16)

    result = None
    for s in range(sections - 1):
        back = to_section(total[s * count : (s + 1) * count], sections - 1, s)
        result = back if result is None else result + back
    return attention_out, result


def solution(mesh):
    return jax.shard_map(
        per_device,
        mesh=mesh,
        in_specs=(
            P(("sec", "dev"), None),
            P(("sec", "dev"), None, None),
            P(("sec", "dev"), None, None, None),
            P(("sec", "dev")),
            P(("sec", "dev"), None),
            P(("sec", "dev"), None),
            P(("sec", "dev"), None),
            P(("sec", "dev"), None, None),
            P(("sec", "dev"), None, None),
        ),
        out_specs=(P(("sec", "dev"), None), P(("sec", "dev"), None)),
        check_vma=False,
    )
```

```python
import functools

import jax
import jax.numpy as jnp
from jax import lax
from jax.experimental import pallas as pl
from jax.experimental.pallas import tpu as pltpu
from jax.sharding import PartitionSpec as P

SIDE = 4
EXTRA = 128
VMEM_LIMIT = 6 << 20


def along(first, distance):
    pairs = []
    for i in range(2 * SIDE * SIDE):
        z, x, core = i // (2 * SIDE), i // 2 % SIDE, i % 2
        if first == (core == 0):
            x = (x + distance) % SIDE
        else:
            z = (z + distance) % SIDE
        pairs.append((i, (z * SIDE + x) * 2 + core))
    return pairs


def step_u(block, distance):
    return lax.ppermute(block, "dev", along(True, distance))


def step_v(block, distance):
    return lax.ppermute(block, "dev", along(False, distance))


def to_section(block, source, target):
    return lax.ppermute(block, "sec", [(source, target)])


def stacked(blocks):
    rows = sum(block.shape[0] for block in blocks)
    start, total = 0, None
    for block in blocks:
        size = block.shape[0]
        padded = jnp.pad(block, ((start, rows - start - size), (0, 0)))
        total = padded if total is None else total + padded
        start += size
    return total


def other_core(block):
    return lax.ppermute(block, "dev", [(i, i ^ 1) for i in range(2 * SIDE * SIDE)])


def attention_block(query, fresh_key_value, kv_cache, cache_lengths):
    count_req = query.shape[0]
    heads_kv = fresh_key_value.shape[1]
    head_size = fresh_key_value.shape[2] // 2
    group_size = query.shape[1] // (heads_kv * head_size)
    query_heads = query.reshape(count_req, heads_kv, group_size, head_size)
    score_scale = head_size ** (-0.5)
    scores = (
        jnp.einsum(
            "rghd,rtgd->rght",
            query_heads,
            kv_cache[..., :head_size],
            preferred_element_type=jnp.float32,
        )
        * score_scale
    )
    valid = jnp.arange(kv_cache.shape[1], dtype=jnp.int32)[None, :] < cache_lengths[:, None]
    scores = jnp.where(valid[:, None, None, :], scores, -jnp.inf)
    own_score = (
        jnp.einsum(
            "rghd,rgd->rgh",
            query_heads,
            fresh_key_value[..., :head_size],
            preferred_element_type=jnp.float32,
        )
        * score_scale
    )
    peak = jnp.maximum(jnp.max(scores, axis=-1), own_score)
    weights = jnp.exp(scores - peak[..., None])
    own_weight = jnp.exp(own_score - peak)
    denominator = jnp.sum(weights, axis=-1) + own_weight
    own_low = lax.optimization_barrier(own_weight.astype(jnp.bfloat16)).astype(jnp.float32)
    mixture = jnp.einsum(
        "rght,rtgd->rghd",
        weights.astype(jnp.bfloat16),
        kv_cache[..., head_size:],
        preferred_element_type=jnp.float32,
    )
    mixture = (
        mixture
        + own_low[..., None] * fresh_key_value[..., head_size:].astype(jnp.float32)[:, :, None, :]
    )
    return (mixture / denominator[..., None]).astype(jnp.bfloat16).reshape(count_req, -1)


def pack_kernel(experts, hidden, routes_in, gates_in, out, routes, gates, sems):
    count, width = hidden.shape
    pairs = ((routes_in, routes), (gates_in, gates), (hidden, out.at[:, :width]))
    copies = [pltpu.make_async_copy(*pair, sems.at[i]) for i, pair in enumerate(pairs)]
    for copy in copies:
        copy.start()
    copies[0].wait()
    copies[1].wait()
    combine = gates[...] / jnp.sum(gates[...], axis=0, keepdims=True)
    place = lax.broadcasted_iota(jnp.int32, (EXTRA, count), 0)
    share = jnp.zeros((EXTRA, count), jnp.float32)
    for k in range(routes.shape[0]):
        named = routes[k : k + 1, :] == place % experts
        share += jnp.where(named, combine[k : k + 1, :], 0.0)
    terms = []
    for _ in range(3):
        terms.append(share.astype(jnp.bfloat16).astype(jnp.float32))
        share = share - terms[-1]
    packed = jnp.where(place < experts, terms[0], jnp.where(place < 2 * experts, terms[1], terms[2]))
    packed = jnp.where(place < 3 * experts, packed, 0.0).astype(jnp.bfloat16)
    same = lax.broadcasted_iota(jnp.int32, (count, count), 0) == lax.broadcasted_iota(
        jnp.int32, (count, count), 1
    )
    turned = lax.dot_general(
        same.astype(jnp.float32).astype(jnp.bfloat16),
        packed,
        (((1,), (1,)), ((), ())),
        preferred_element_type=jnp.float32,
    )
    out[:, width:] = turned.astype(jnp.bfloat16)
    copies[2].wait()


def token_rows(hidden, routes, gates, experts):
    count, width = hidden.shape
    whole = pl.BlockSpec(memory_space=pltpu.VMEM)
    return pl.pallas_call(
        functools.partial(pack_kernel, experts),
        in_specs=[pl.BlockSpec(memory_space=pl.ANY)] * 3,
        out_specs=whole,
        out_shape=jax.ShapeDtypeStruct((count, width + EXTRA), hidden.dtype),
        scratch_shapes=[
            pltpu.VMEM(routes.shape[::-1], routes.dtype),
            pltpu.VMEM(gates.shape[::-1], gates.dtype),
            pltpu.SemaphoreType.DMA((3,)),
        ],
        compiler_params=pltpu.CompilerParams(vmem_limit_bytes=VMEM_LIMIT),
    )(*(pltpu.with_memory_space_constraint(w, pltpu.HBM) for w in (hidden, routes.T, gates.T)))


def weight_copies(gate_up, down, kept, sems):
    inner = down.shape[0]
    sources = (gate_up.at[:, :inner], gate_up.at[:, inner:], down)
    return [pltpu.make_async_copy(*pair, sems.at[i]) for i, pair in enumerate(zip(sources, kept))]


def kept_shapes(gate_up, down):
    inner, width = down.shape
    shapes = [(width, inner), (width, inner), (inner, width)]
    return [pltpu.VMEM(shape, down.dtype) for shape in shapes]


def expert_kernel(pieces, columns, load, serving, *refs):
    @pl.when(serving[0] > 0)
    def _():
        expert_rows(pieces, columns, load, *refs)


def expert_rows(pieces, columns, load, *refs):
    refs = list(refs)
    pick = refs.pop(0)
    rows_in = [refs.pop(0) for _ in range(pieces)]
    halves = [[refs.pop(0) for _ in range(2 if load else 3)] for _ in range(2)]
    outs = [refs.pop(0) for _ in range(pieces)]
    copies = []
    if load:
        kept = [[refs.pop(0) for _ in range(3)] for _ in range(2)]
        sems = refs.pop()
        for half in range(2):
            copies += weight_copies(*halves[half], kept[half], sems.at[half])
        halves = kept
        for index in (0, 1, 3, 4, 2, 5):
            copies[index].start()
    rows, act, share = refs
    inner, width = halves[0][2].shape

    def arrived(index):
        if load:
            copies[index].wait()

    start = 0
    for ref in rows_in:
        size = ref.shape[0]
        rows[start : start + size, :] = ref[:, :width]
        share[start : start + size, :] = jnp.sum(
            ref[:, width:].astype(jnp.float32) * pick[...], axis=1, keepdims=True
        )
        start += size

    for half, (gate, up, _) in enumerate(halves):
        arrived(3 * half)
        left = jnp.dot(rows[...], gate[...], preferred_element_type=jnp.float32)
        arrived(3 * half + 1)
        right = jnp.dot(rows[...], up[...], preferred_element_type=jnp.float32)
        act[:, half * inner : (half + 1) * inner] = (jax.nn.silu(left) * right).astype(jnp.bfloat16)
    arrived(2)
    arrived(5)

    @pl.loop(0, width // columns)
    def _(n):
        at = pl.ds(pl.multiple_of(n * columns, columns), columns)
        total = jnp.dot(act[:, :inner], halves[0][2][:, at], preferred_element_type=jnp.float32)
        total += jnp.dot(act[:, inner:], halves[1][2][:, at], preferred_element_type=jnp.float32)
        total = (total * share[...]).astype(jnp.bfloat16)
        start = 0
        for out in outs:
            out[:, at] = total[start : start + out.shape[0], :]
            start += out.shape[0]


def experts_on(pieces, serving, pick, halves):
    inner, width = halves[0][-1].shape
    load = len(halves[0]) == 2
    sizes = [piece.shape[0] for piece in pieces]
    count = sum(sizes)
    whole = pl.BlockSpec(memory_space=pltpu.VMEM)
    space = pl.BlockSpec(memory_space=pl.ANY) if load else whole
    constraint = pltpu.HBM if load else pltpu.VMEM
    held = [pltpu.with_memory_space_constraint(w, constraint) for half in halves for w in half]
    kept = [shape for half in halves for shape in kept_shapes(*half)] if load else []
    outs = pl.pallas_call(
        functools.partial(expert_kernel, len(pieces), 1024, load),
        in_specs=[pl.BlockSpec(memory_space=pltpu.SMEM)] + [whole] * (1 + len(pieces)) + [space] * len(held),
        out_specs=[whole] * (len(sizes) + len(kept)),
        out_shape=[jax.ShapeDtypeStruct((size, width), jnp.bfloat16) for size in sizes] + kept,
        scratch_shapes=[
            pltpu.VMEM((count, width), jnp.bfloat16),
            pltpu.VMEM((count, 2 * inner), jnp.bfloat16),
            pltpu.VMEM((count, 1), jnp.float32),
        ]
        + ([pltpu.SemaphoreType.DMA((2, 3))] if load else []),
        compiler_params=pltpu.CompilerParams(vmem_limit_bytes=VMEM_LIMIT),
        cost_estimate=pl.CostEstimate(
            flops=12 * count * width * inner,
            bytes_accessed=12 * width * inner if load else 4 * count * width,
            transcendentals=2 * count * inner,
        ),
    )(serving, pick, *(pltpu.with_memory_space_constraint(w, pltpu.VMEM) for w in pieces), *held)
    kept = outs[len(sizes) :]
    return outs[: len(sizes)], (kept[:3], kept[3:]) if load else halves


def per_device(
    query, fresh_key_value, kv_cache, cache_lengths, hidden, routes, gates, w_gate_up, w_down
):
    sections = lax.axis_size("sec")
    section = lax.axis_index("sec")
    experts = lax.axis_size("dev") // 2
    expert = lax.axis_index("dev") // 2
    expert_side = section == sections - 1
    count = hidden.shape[0]
    f32 = jnp.float32

    gate_up, down = w_gate_up[0], w_down[0]
    halves = ((gate_up, down), (other_core(gate_up), other_core(down)))

    packed = token_rows(hidden, routes, gates, experts)
    blocks = [to_section(packed, s, sections - 1) for s in range(sections - 1)]
    block = jnp.concatenate(blocks, axis=0)

    held = block.shape[0]
    size = SIDE * held
    cut = 16 * ((size // 2 + 15) // 16)
    lead = cut - 2 * held
    behind, ahead = step_u(block, 1), step_u(block, -1)
    block, behind, ahead = lax.optimization_barrier((block, behind, ahead))
    far = step_u(block, 2)
    group_a, group_b = stacked([block, behind, ahead[:lead]]), stacked([ahead[lead:], far])
    before_a, after_b = step_v(group_a, 1), step_v(group_b, -1)
    before_b, after_a = step_v(group_b, 1), step_v(group_a, -1)
    column = lax.broadcasted_iota(jnp.int32, (1, EXTRA), 1)
    pick = ((column % experts == expert) & (column < 3 * experts)).astype(f32)
    serving = expert_side.astype(jnp.int32).reshape(1)
    (own_a, own_b), halves = experts_on([group_a, group_b], serving, pick, halves)

    before_a, after_b, before_b, after_a, own_a, own_b = lax.optimization_barrier(
        (before_a, after_b, before_b, after_a, own_a, own_b)
    )
    across_a, across_b = step_v(before_a, 1), step_v(after_b, -1)
    (after_b, before_a), _ = experts_on([after_b, before_a], serving, pick, halves)
    across_a, across_b, after_b, before_a = lax.optimization_barrier((across_a, across_b, after_b, before_a))

    from_after_b, from_before_a = step_v(after_b, 1), step_v(before_a, -1)
    (cross_a, cross_b), _ = experts_on([across_a, across_b], serving, pick, halves)
    from_cross_a, from_cross_b = step_v(cross_a, 1), step_v(cross_b, -1)
    after_a, before_b, from_after_b, from_before_a, cross_a = lax.optimization_barrier(
        (after_a, before_b, from_after_b, from_before_a, cross_a)
    )
    (after_a, before_b), _ = experts_on([after_a, before_b], serving, pick, halves)

    query, _ = lax.optimization_barrier((query, cross_a))
    attention_out = lax.cond(
        expert_side,
        lambda query, *_: jnp.zeros_like(query),
        attention_block,
        query,
        fresh_key_value,
        kv_cache,
        cache_lengths,
    )

    from_before_b = step_v((before_b.astype(f32) + from_cross_b.astype(f32)).astype(jnp.bfloat16), -1)
    from_after_a = step_v((after_a.astype(f32) + from_cross_a.astype(f32)).astype(jnp.bfloat16), 1)
    near = held - lead
    sum_b = own_b.astype(f32) + from_after_b.astype(f32) + from_before_b.astype(f32)
    far = sum_b[near:].astype(jnp.bfloat16)
    part = held // 2
    from_far_a, from_far_b = step_u(far[:part], 1), step_u(far[part:], -1)
    sum_a = own_a.astype(f32) + from_after_a.astype(f32) + from_before_a.astype(f32)
    ahead = jnp.concatenate([sum_a[2 * held :], sum_b[:near]], axis=0)
    ahead = ahead + jnp.pad(from_far_a.astype(f32), ((0, held - part), (0, 0)))
    behind = sum_a[held : 2 * held] + jnp.pad(from_far_b.astype(f32), ((part, 0), (0, 0)))
    total = (
        sum_a[:held]
        + step_u(ahead.astype(jnp.bfloat16), 1).astype(f32)
        + step_u(behind.astype(jnp.bfloat16), -1).astype(f32)
    ).astype(jnp.bfloat16)

    result = None
    for s in range(sections - 1):
        back = to_section(total[s * count : (s + 1) * count], sections - 1, s)
        result = back if result is None else result + back
    return attention_out, result


def solution(mesh):
    return jax.shard_map(
        per_device,
        mesh=mesh,
        in_specs=(
            P(("sec", "dev"), None),
            P(("sec", "dev"), None, None),
            P(("sec", "dev"), None, None, None),
            P(("sec", "dev")),
            P(("sec", "dev"), None),
            P(("sec", "dev"), None),
            P(("sec", "dev"), None),
            P(("sec", "dev"), None, None),
            P(("sec", "dev"), None, None),
        ),
        out_specs=(P(("sec", "dev"), None), P(("sec", "dev"), None)),
        check_vma=False,
    )
```
